32 devices in a mesh: edge: 8 (over z, x), feat: 4 (over y, core).
Axes of the slice: x: 2, y: 2, z: 4, core: 2. Of those that a mesh axis runs over, the one named last changes fastest.
Arguments:
- node_feat: bfloat16 [16384, 128], P('edge'), may hold values from -6 to 6
- cotangent: bfloat16 [16384, 128], P('edge'), may hold values from -6 to 6
- w_msg: bfloat16 [128, 128], replicated, may hold values from -0.5 to 0.5
- w_self: bfloat16 [128, 128], replicated, may hold values from -0.5 to 0.5
- adjacency: bfloat16 [8, 4, 64, 128, 128], P('edge', 'feat'), may hold values from -0.125 to 0.125
- edge_src: int32 [8, 4, 64], P('edge', 'feat'), may hold values from 0 to 15
- edge_dst: int32 [8, 4, 64], P('edge', 'feat'), may hold values from 0 to 15
- send_src: int32 [8, 4, 8, 2], P('edge', 'feat'), may hold values from 0 to 15
- recv_dst: int32 [8, 4, 8, 2], P('edge', 'feat'), may hold values from 0 to 15
- live: int32 [8, 4], P('edge', 'feat'), may hold values from 4 to 64, as said below
Outputs:
- out_feat: bfloat16 [16384, 128], P('edge')
- grad_feat: bfloat16 [16384, 128], P('edge')
- grad_wmsg: float32 [128, 128], replicated
- grad_wself: float32 [128, 128], replicated
The draws below stay inside these ranges and needn't reach their ends.
Inputs may be any that keep to these rules, and one draw needn't show every extreme that they name: Each device has between 64 // 16 (at least 1) and 64 live blocks; one device always has all 64 live.
All inputs are finite; a program needn't handle non-finite values.
Results may differ from the reference program's by a relative error of at most 0.0054.
Values may be sent and summed in bfloat16 or wider, within the bound.
No kernel may reach another device: no remote copies, remote signals or barrier semaphores. Data moves between devices by JAX's collectives and lax.ppermute only.
A program may use at most 128 MiB of HBM per device.

```python
import jax
import jax.numpy as jnp
from jax import lax

H = 128
BLK = 128
NB_DEV = 16
EB_DEV = 64
CAPS = 2
CAPD = 2
NODES = 16384
N_EDGE = 8
N_FEAT = 4


def draw_live(key, part):
    base = jax.random.randint(key, (N_EDGE * N_FEAT,), max(1, EB_DEV // 16), EB_DEV + 1)
    chosen = jax.random.randint(jax.random.fold_in(key, 7), (), 0, N_EDGE * N_FEAT)
    filled = jnp.where(jnp.arange(N_EDGE * N_FEAT, dtype=jnp.int32) == chosen, EB_DEV, base)
    return filled.reshape(N_EDGE, N_FEAT).astype(jnp.int32)


def with_ends(entries, own_key, least, top_value):
    shape = entries.shape
    spot = [jax.random.randint(jax.random.fold_in(own_key, axis), (), 0, shape[axis]) for axis in range(len(shape))]
    entries = entries.at[tuple(spot)].set(least)
    longest = shape.index(max(shape))
    spot[longest] = (spot[longest] + 1) % shape[longest]
    return entries.at[tuple(spot)].set(top_value)


def shard_levels(key, extent, pieces, smallest, high):
    loudness = 1.0
    for axis_at, parts in pieces:
        heights = jax.random.uniform(jax.random.fold_in(jax.random.fold_in(key, 6), axis_at), (parts,), jnp.float32, smallest / len(pieces), high / len(pieces))
        loudness = loudness * jnp.repeat(jnp.exp(heights), extent[axis_at] // parts).reshape((-1,) + (1,) * (len(extent) - 1 - axis_at))
    return loudness


def bell_draw(stream_key, dims, scale, most, shards=(), held_as=jnp.bfloat16):
    values = jax.random.normal(stream_key, dims, jnp.float32) * scale
    if len(shards) > 0:
        values = shard_levels(stream_key, dims, shards, -0.22, 0.18) * values
    return jnp.clip(values, min=-most, max=most).astype(held_as)


def setup_inputs(seed: int = 0) -> dict:
    splits = jax.random.split(jax.random.key(seed), 11)
    node_feat = bell_draw(splits[0], (NODES, H), 1.0, 6.0, ((0, 8),))
    cotangent = bell_draw(splits[1], (NODES, H), 1.0, 6.0, ((0, 8),))
    w_msg = bell_draw(splits[2], (H, H), H ** -0.5, 0.5)
    w_self = bell_draw(splits[3], (H, H), H ** -0.5, 0.5)
    adjacency = bell_draw(splits[4], (N_EDGE, N_FEAT, EB_DEV, BLK, BLK), (BLK * EB_DEV * N_FEAT // NB_DEV) ** -0.5, 0.125, ((0, 8), (1, 4)))
    edge_src = with_ends(jax.random.randint(splits[5], (N_EDGE, N_FEAT, EB_DEV), 0, N_EDGE * CAPS), jax.random.fold_in(splits[5], 1), 0, (N_EDGE * CAPS) - 1).astype(jnp.int32)
    edge_dst = with_ends(jax.random.randint(splits[6], (N_EDGE, N_FEAT, EB_DEV), 0, N_EDGE * CAPD), jax.random.fold_in(splits[6], 1), 0, (N_EDGE * CAPD) - 1).astype(jnp.int32)
    send_src = with_ends(jax.random.randint(splits[7], (N_EDGE, N_FEAT, N_EDGE, CAPS), 0, NB_DEV), jax.random.fold_in(splits[7], 1), 0, NB_DEV - 1).astype(jnp.int32)
    recv_dst = with_ends(jax.random.randint(splits[8], (N_EDGE, N_FEAT, N_EDGE, CAPD), 0, NB_DEV), jax.random.fold_in(splits[8], 1), 0, NB_DEV - 1).astype(jnp.int32)
    live = draw_live(jax.random.fold_in(splits[10], 71), 0)
    return dict(node_feat=node_feat, cotangent=cotangent, w_msg=w_msg, w_self=w_self, adjacency=adjacency, edge_src=edge_src, edge_dst=edge_dst, send_src=send_src, recv_dst=recv_dst, live=live)


def reference(node_feat, cotangent, w_msg, w_self, adjacency, edge_src, edge_dst, send_src, recv_dst, live):
    block_total = NB_DEV * N_EDGE
    device_total = N_EDGE * N_FEAT
    feat_index = jnp.arange(N_FEAT, dtype=jnp.int32)[None, :, None]
    edge_index = jnp.arange(N_EDGE, dtype=jnp.int32)[:, None, None]
    src_peer = edge_src // CAPS
    src_glob = src_peer * NB_DEV + send_src[src_peer, feat_index, edge_index, edge_src % CAPS]
    dst_owner = edge_dst // CAPD
    dst_glob = dst_owner * NB_DEV + recv_dst[dst_owner, feat_index, edge_index, edge_dst % CAPD]
    keep_mask = (jnp.arange(EB_DEV, dtype=jnp.int32)[None, None, :] < live[:, :, None]).astype(jnp.float32)
    blocks_all = adjacency.reshape(device_total, EB_DEV, BLK, BLK)
    src_flat = src_glob.reshape(device_total, EB_DEV).astype(jnp.int32)
    dst_flat = dst_glob.reshape(device_total, EB_DEV).astype(jnp.int32)
    keep_flat = keep_mask.reshape(device_total, EB_DEV)

    messages = jnp.dot(node_feat, w_msg, preferred_element_type=jnp.float32).astype(jnp.bfloat16)
    message_blocks = messages.reshape(block_total, BLK, H)

    def forward_step(running, scan_item):
        blocks, src_ids, dst_ids, keep_rows = scan_item
        terms = jnp.einsum("eij,ejh->eih", blocks.astype(jnp.float32), message_blocks[src_ids].astype(jnp.float32))
        terms = terms * keep_rows[:, None, None]
        return running.at[dst_ids].add(terms), None

    aggregate, _ = lax.scan(forward_step, jnp.zeros((block_total, BLK, H), jnp.float32), (blocks_all, src_flat, dst_flat, keep_flat))
    preact = jnp.dot(node_feat, w_self, preferred_element_type=jnp.float32) + aggregate.reshape(-1, H)
    sigmoid_pre = jax.nn.sigmoid(preact)
    out_feat = (preact * sigmoid_pre).astype(jnp.bfloat16)
    grad_pre = (cotangent.astype(jnp.float32) * sigmoid_pre * (1.0 + preact * (1.0 - sigmoid_pre))).astype(jnp.bfloat16)
    grad_wself = jnp.dot(node_feat.T, grad_pre, preferred_element_type=jnp.float32)
    grad_blocks = grad_pre.reshape(block_total, BLK, H)

    def backward_step(running, scan_item):
        blocks, src_ids, dst_ids, keep_rows = scan_item
        terms = jnp.einsum("eij,eih->ejh", blocks.astype(jnp.float32), grad_blocks[dst_ids].astype(jnp.float32))
        terms = terms * keep_rows[:, None, None]
        return running.at[src_ids].add(terms), None

    grad_sum, _ = lax.scan(backward_step, jnp.zeros((block_total, BLK, H), jnp.float32), (blocks_all, src_flat, dst_flat, keep_flat))
    grad_msg = grad_sum.reshape(-1, H).astype(jnp.bfloat16)
    grad_wmsg = jnp.dot(node_feat.T, grad_msg, preferred_element_type=jnp.float32)
    grad_feat = (jnp.dot(grad_pre, w_self.T, preferred_element_type=jnp.float32) + jnp.dot(grad_msg, w_msg.T, preferred_element_type=jnp.float32)).astype(jnp.bfloat16)
    return out_feat, grad_feat, grad_wmsg, grad_wself
```

```python
import functools
import math

import jax
import jax.numpy as jnp
from jax import lax
from jax.experimental import pallas as pl
from jax.experimental.pallas import tpu as pltpu
from jax.sharding import PartitionSpec as P

BOTH = ("edge", "feat")
F32 = jnp.float32
BF16 = jnp.bfloat16
VMEM = pl.BlockSpec(memory_space=pltpu.VMEM)
SMEM = pl.BlockSpec(memory_space=pltpu.SMEM)


def is_pow2(n):
    return n & (n - 1) == 0


def swap(x, axis, bit):
    size = lax.axis_size(axis)
    return lax.ppermute(x, axis, [(j, j ^ bit) for j in range(size)])


def gather_feat(x):
    size = lax.axis_size("feat")
    if not is_pow2(size):
        return lax.all_gather(x, "feat", axis=0)
    me = lax.axis_index("feat")
    held = x[None]
    bit = 1
    while bit < size:
        other = swap(held, "feat", bit)
        mine_low = (me & bit) == 0
        held = jnp.where(
            mine_low, jnp.concatenate([held, other], 0), jnp.concatenate([other, held], 0)
        )
        bit *= 2
    return held


def sum_all(x):
    for axis in ("feat", "edge"):
        size = lax.axis_size(axis)
        if not is_pow2(size):
            x = lax.psum(x, axis)
            continue
        bit = 1
        while bit < size:
            x = x + swap(x, axis, bit)
            bit *= 2
    return x


def pick_kernel(ids, rows, out):
    for i in range(out.shape[0]):
        out[i] = rows[ids[i]]


def forward_kernel(group, live, src, dst, raw, w_msg, adj, out, msgs, acc):
    slots, block, hidden = raw.shape
    per_owner, width = out.shape[1:3]
    planes = block // width
    flat = raw[...].reshape(slots * block, hidden)
    msgs[...] = (
        jnp.dot(flat, w_msg[...], preferred_element_type=F32)
        .astype(BF16)
        .reshape(slots, block, hidden)
    )
    acc[...] = jnp.zeros_like(acc)
    count = live[0]

    def step(turn, carry):
        terms = []
        for u in range(group):
            k = turn * group + u
            terms.append(jnp.dot(adj[k], msgs[src[k]], preferred_element_type=F32))
        for u in range(group):
            k = turn * group + u
            d = jnp.where(k < count, dst[k], slots)
            acc[d] += terms[u]
        return carry

    lax.fori_loop(0, (count + group - 1) // group, step, 0)
    for s in range(slots):
        for q in range(planes):
            out[s // per_owner * planes + q, s % per_owner] = acc[
                s, q * width : (q + 1) * width
            ].astype(BF16)


def owner_kernel(
    me, ids, got, feat, cot, w_self, out_feat, grad_pre, outgoing, w_part, agg, held
):
    blocks, planes, width, hidden = feat.shape
    devices, per_owner = got.shape[:2]
    q = me[0]
    agg[...] = jnp.zeros_like(agg)
    for i in range(devices):
        for j in range(per_owner):
            agg[ids[i * per_owner + j]] += got[i, j].astype(F32)
    mine = feat[:, q].reshape(blocks * width, hidden)
    preact = jnp.dot(mine, w_self[...], preferred_element_type=F32)
    preact = preact + agg[...].reshape(blocks * width, hidden)
    sig = jax.nn.sigmoid(preact)
    out_feat[...] = (preact * sig).astype(BF16).reshape(blocks, width, hidden)
    grad = cot[:, q].reshape(blocks * width, hidden).astype(F32)
    grad = (grad * sig * (1.0 + preact * (1.0 - sig))).astype(BF16)
    held[...] = grad.reshape(blocks, width, hidden)
    grad_pre[...] = held[...]
    for i in range(devices):
        for j in range(per_owner):
            outgoing[i, j] = held[ids[i * per_owner + j]]
    w_part[...] = lax.dot_general(
        mine, grad, (((0,), (0,)), ((), ())), preferred_element_type=F32
    )


def backward_kernel(group, live, src, dst, got, raw, adj, out, w_part, turned, acc):
    slots, block, hidden = raw.shape
    devices, per_owner, width = got.shape[:3]
    planes = block // width
    out_slots = out.shape[1]
    for p in range(devices // planes):
        for j in range(per_owner):
            whole = jnp.concatenate([got[p * planes + q, j] for q in range(planes)], 0)
            turned[p * per_owner + j] = whole.T
    acc[...] = jnp.zeros_like(acc)
    count = live[0]

    def step(turn, carry):
        terms = []
        for u in range(group):
            k = turn * group + u
            terms.append(jnp.dot(turned[dst[k]], adj[k], preferred_element_type=F32))
        for u in range(group):
            k = turn * group + u
            s = jnp.where(k < count, src[k], slots)
            acc[s] += terms[u]
        return carry

    lax.fori_loop(0, (count + group - 1) // group, step, 0)
    total = jnp.zeros((hidden, hidden), F32)
    for s in range(slots):
        term = acc[s]
        total += jnp.dot(term.astype(BF16), raw[s], preferred_element_type=F32)
        back = term.T.astype(BF16)
        for q in range(planes):
            out[s // out_slots * planes + q, s % out_slots] = back[
                q * width : (q + 1) * width
            ]
    w_part[...] = total.T


def last_kernel(ids, got, grad_pre, w_self, w_msg, out, agg):
    blocks, width, hidden = grad_pre.shape
    devices, per_owner = got.shape[:2]
    agg[...] = jnp.zeros_like(agg)
    for i in range(devices):
        for j in range(per_owner):
            agg[ids[i * per_owner + j]] += got[i, j].astype(F32)
    grad_msg = agg[...].reshape(blocks * width, hidden).astype(BF16)
    turn = (((1,), (1,)), ((), ()))
    total = lax.dot_general(
        grad_pre[...].reshape(blocks * width, hidden),
        w_self[...],
        turn,
        preferred_element_type=F32,
    ) + lax.dot_general(grad_msg, w_msg[...], turn, preferred_element_type=F32)
    out[...] = total.astype(BF16).reshape(blocks, width, hidden)


def shape(dims, dtype):
    return jax.ShapeDtypeStruct(dims, dtype)


def body(
    node_feat, cotangent, w_msg, w_self, adjacency, edge_src, edge_dst, send_src, recv_dst, live
):
    block = adjacency.shape[-1]
    hidden = node_feat.shape[1]
    blocks = node_feat.shape[0] // block
    peers = lax.axis_size("edge")
    planes = lax.axis_size("feat")
    devices = peers * planes
    width = block // planes
    n_send = send_src.shape[-1]
    n_recv = recv_dst.shape[-1]
    adj = adjacency.reshape(-1, block, block)
    src = edge_src.reshape(-1)
    dst = edge_dst.reshape(-1)
    count = live.reshape(1)
    group = math.gcd(4, adj.shape[0])
    me = lax.axis_index("feat").reshape(1).astype(jnp.int32)
    params = pltpu.CompilerParams(vmem_limit_bytes=32 * 2**20)

    ids = jnp.concatenate([send_src.reshape(peers, n_send), recv_dst.reshape(peers, n_recv)], 1)
    ids = gather_feat(ids).transpose(1, 0, 2)
    send_all = ids[:, :, :n_send].reshape(-1)
    recv_all = ids[:, :, n_send:].reshape(-1)

    outgoing = pl.pallas_call(
        pick_kernel,
        out_shape=shape((peers * n_send, block, hidden), BF16),
        in_specs=[SMEM, VMEM],
        out_specs=VMEM,
        compiler_params=params,
        name="pick_rows",
    )(send_src.reshape(-1), node_feat.reshape(blocks, block, hidden))
    raw = lax.all_to_all(outgoing, "edge", 0, 0, tiled=True)

    partials = pl.pallas_call(
        functools.partial(forward_kernel, group),
        out_shape=shape((devices, n_recv, width, hidden), BF16),
        in_specs=[SMEM] * 3 + [VMEM] * 3,
        out_specs=VMEM,
        scratch_shapes=[
            pltpu.VMEM((peers * n_send, block, hidden), BF16),
            pltpu.VMEM((peers * n_recv + 1, block, hidden), F32),
        ],
        compiler_params=params,
        name="edge_forward",
    )(count, src, dst, raw, w_msg, adj)
    got = lax.all_to_all(partials, BOTH, 0, 0, tiled=True)

    quarter = shape((blocks, width, hidden), BF16)
    out_part, grad_pre, grad_out, wself_part = pl.pallas_call(
        owner_kernel,
        out_shape=(
            quarter,
            quarter,
            shape((devices, n_recv, width, hidden), BF16),
            shape((hidden, hidden), F32),
        ),
        in_specs=[SMEM] * 2 + [VMEM] * 4,
        out_specs=(VMEM,) * 4,
        scratch_shapes=[
            pltpu.VMEM((blocks, width, hidden), F32),
            pltpu.VMEM((blocks, width, hidden), BF16),
        ],
        compiler_params=params,
        name="owner_dense",
    )(
        me,
        recv_all,
        got,
        node_feat.reshape(blocks, planes, width, hidden),
        cotangent.reshape(blocks, planes, width, hidden),
        w_self,
    )
    grad_in = lax.all_to_all(grad_out, BOTH, 0, 0, tiled=True)
    out_feat = gather_feat(out_part).transpose(1, 0, 2, 3).reshape(-1, hidden)

    grad_partials, wmsg_part = pl.pallas_call(
        functools.partial(backward_kernel, group),
        out_shape=(
            shape((devices, n_send, width, hidden), BF16),
            shape((hidden, hidden), F32),
        ),
        in_specs=[SMEM] * 3 + [VMEM] * 3,
        out_specs=(VMEM,) * 2,
        scratch_shapes=[
            pltpu.VMEM((peers * n_recv, hidden, block), BF16),
            pltpu.VMEM((peers * n_send + 1, hidden, block), F32),
        ],
        compiler_params=params,
        name="edge_backward",
    )(count, src, dst, grad_in, raw, adj)
    grad_back = lax.all_to_all(grad_partials, BOTH, 0, 0, tiled=True)
    grad_wself = sum_all(wself_part)
    grad_wmsg = sum_all(wmsg_part)

    grad_part = pl.pallas_call(
        last_kernel,
        out_shape=quarter,
        in_specs=[SMEM] + [VMEM] * 4,
        out_specs=VMEM,
        scratch_shapes=[pltpu.VMEM((blocks, width, hidden), F32)],
        compiler_params=params,
        name="owner_last",
    )(send_all, grad_back, grad_pre, w_self, w_msg)
    grad_feat = gather_feat(grad_part).transpose(1, 0, 2, 3).reshape(-1, hidden)
    return (out_feat, grad_feat, grad_wmsg, grad_wself)


def solution(mesh):
    in_specs = (
        P("edge", None),
        P("edge", None),
        P(),
        P(),
        P("edge", "feat", None, None, None),
        P("edge", "feat", None),
        P("edge", "feat", None),
        P("edge", "feat", None, None),
        P("edge", "feat", None, None),
        P("edge", "feat"),
    )
    out_specs = (P("edge", None), P("edge", None), P(), P())
    return jax.shard_map(body, mesh=mesh, in_specs=in_specs, out_specs=out_specs, check_vma=False)
```

```python
import functools
import math

import jax
import jax.numpy as jnp
from jax import lax
from jax.experimental import pallas as pl
from jax.experimental.pallas import tpu as pltpu
from jax.sharding import PartitionSpec as P

BOTH = ("edge", "feat")
F32 = jnp.float32
BF16 = jnp.bfloat16
VMEM = pl.BlockSpec(memory_space=pltpu.VMEM)
SMEM = pl.BlockSpec(memory_space=pltpu.SMEM)
HBM = pl.BlockSpec(memory_space=pltpu.HBM)
ANY = pl.BlockSpec(memory_space=pl.ANY)


def is_pow2(n):
    return n & (n - 1) == 0


def swap(x, axis, bit):
    size = lax.axis_size(axis)
    return lax.ppermute(x, axis, [(j, j ^ bit) for j in range(size)])


def gather_feat(x):
    size = lax.axis_size("feat")
    if not is_pow2(size):
        return lax.all_gather(x, "feat", axis=0)
    me = lax.axis_index("feat")
    held = x[None]
    bit = 1
    while bit < size:
        other = swap(held, "feat", bit)
        mine_low = (me & bit) == 0
        held = jnp.where(
            mine_low, jnp.concatenate([held, other], 0), jnp.concatenate([other, held], 0)
        )
        bit *= 2
    return held


def pieces_feat(x, beside=None):
    bit = lax.axis_size("feat") // 2
    held = {0: x}
    other = None if beside is None else swap_all(beside, 1)
    while bit:
        held.update({m | bit: swap(v, "feat", bit) for m, v in held.items()})
        if other is not None:
            held, other = lax.optimization_barrier((held, other))
        bit //= 2
    return [held[m] for m in sorted(held)], other


def join_kernel(planes, me, *refs):
    parts, refs = refs[:planes], refs[planes:]
    halves, (out, *sums, sems) = (refs[:2], refs[2:]) if len(refs) > 2 else ((), refs)
    copies = [
        pltpu.make_async_copy(part, out.at[:, me[0] ^ m], sems.at[m])
        for m, part in enumerate(parts)
    ]
    for n, total in enumerate(sums):
        rows = total.shape[1]
        copies += [
            pltpu.make_async_copy(
                half.at[n * rows : (n + 1) * rows],
                total.at[(me[0] & 1) ^ m],
                sems.at[planes + 2 * n + m],
            )
            for m, half in enumerate(halves)
        ]
    for copy in copies:
        copy.start()
    for copy in copies:
        copy.wait()


def join_feat(x, me, params, sums=None):
    blocks, width, hidden = x.shape
    planes = lax.axis_size("feat")
    pieces, other = pieces_feat(x, sums)
    out_shape = [pltpu.HBM((blocks, planes, width, hidden), BF16)]
    if sums is not None:
        count = 2 * sums.shape[0] // hidden
        out_shape += [pltpu.HBM((2, hidden // 2, hidden), F32)] * count
        pieces = pieces + [sums, other]
    joined = pl.pallas_call(
        functools.partial(join_kernel, planes),
        out_shape=out_shape,
        in_specs=[SMEM] + [VMEM] * len(pieces),
        out_specs=[HBM] * len(out_shape),
        scratch_shapes=[pltpu.SemaphoreType.DMA((planes + 2 * len(out_shape),))],
        compiler_params=params,
        name="join_rows",
    )(me, *pieces)
    return [v.reshape(-1, hidden) for v in joined]


def stages_of(count):
    bits = [1 << n for n in range(count.bit_length() - 1)]
    return [bits[:1]] + [bits[n : n + 2] for n in range(1, len(bits), 2)]


def swap_all(x, mask):
    count = lax.axis_size(BOTH)
    return lax.ppermute(x, BOTH, [(j, j ^ mask) for j in range(count)])


def sum_stage(x, bits):
    terms = {0: x}
    for bit in bits:
        terms.update({m | bit: swap_all(x, m | bit) for m in list(terms)})
    held = [terms[m].astype(F32) for m in sorted(terms)]
    while len(held) > 1:
        held = [held[n] + held[n + 1] for n in range(0, len(held), 2)]
    return held[0]


def split_core(x, me):
    halves = x.reshape(2, -1, x.shape[-1])
    low = (me & 1) == 0
    mine = jnp.where(low, halves[0], halves[1])
    other = jnp.where(low, halves[1], halves[0])
    return mine + swap_all(other, 1)


def pick_kernel(ids, rows, w_msg, w_self, out, w_msg_out, w_self_out, room, sems, out_sems):
    n_send, peers = ids.shape
    count = peers * n_send
    ins = [
        pltpu.make_async_copy(
            rows.at[ids[j, p]], room.at[p * n_send + j], sems.at[p * n_send + j]
        )
        for p in range(peers)
        for j in range(n_send)
    ]
    others = [
        pltpu.make_async_copy(w_msg, w_msg_out, sems.at[count]),
        pltpu.make_async_copy(w_self, w_self_out, sems.at[count + 1]),
    ]
    outs = [pltpu.make_async_copy(room.at[i], out.at[i], out_sems.at[i]) for i in range(count)]
    for copy in ins + others:
        copy.start()
    for one, two in zip(ins, outs):
        one.wait()
        two.start()
    for copy in others + outs:
        copy.wait()


def edge_loop(group, count, adj, held, sems, term, put):
    chunks = sems.shape[0]
    size = held.shape[0] // chunks
    copies = [
        pltpu.make_async_copy(
            adj.at[c * size : (c + 1) * size], held.at[c * size : (c + 1) * size], sems.at[c]
        )
        for c in range(chunks)
    ]

    def start():
        for copy in copies:
            copy.start()

    def run():
        for c, copy in enumerate(copies):
            copy.wait()

            def step(turn, carry, first=c * size):
                ks = [first + turn * group + u for u in range(group)]
                terms = [term(k) for k in ks]
                for k, value in zip(ks, terms):
                    put(k, k < count, value)
                return carry

            left = jnp.clip(count - c * size, 0, size)
            lax.fori_loop(0, (left + group - 1) // group, step, 0)

    return start, run


def send_out(room, out, sems, p, size):
    copy = pltpu.make_async_copy(
        room.at[p * size : (p + 1) * size], out.at[p * size : (p + 1) * size], sems.at[p]
    )
    copy.start()
    return copy


def forward_kernel(
    group,
    live,
    me,
    src,
    dst,
    raw,
    w_msg,
    adj,
    feat,
    cot,
    out,
    feat_out,
    cot_out,
    msgs,
    acc,
    held,
    room,
    sems,
    more_sems,
    out_sems,
):
    slots, block, hidden = raw.shape
    per_owner, width = out.shape[1:3]
    planes = block // width

    def term(k):
        return jnp.dot(held[k], msgs[src[k]], preferred_element_type=F32)

    def put(k, alive, value):
        acc[jnp.where(alive, dst[k], slots)] += value

    start, run = edge_loop(group, live[0], adj, held, sems, term, put)
    start()
    parts = [
        pltpu.make_async_copy(feat.at[:, me[0]], feat_out, more_sems.at[0]),
        pltpu.make_async_copy(cot.at[:, me[0]], cot_out, more_sems.at[1]),
    ]
    for copy in parts:
        copy.start()
    flat = raw[...].reshape(slots * block, hidden)
    msgs[...] = (
        jnp.dot(flat, w_msg[...], preferred_element_type=F32)
        .astype(BF16)
        .reshape(slots, block, hidden)
    )
    acc[...] = jnp.zeros_like(acc)
    run()
    for p in range(out.shape[0] // planes):
        for j in range(per_owner):
            for q in range(planes):
                room[p * planes + q, j] = acc[
                    p * per_owner + j, q * width : (q + 1) * width
                ].astype(BF16)
        parts.append(send_out(room, out, out_sems, p, planes))
    for copy in parts:
        copy.wait()


def owner_kernel(
    ids, got, feat, cot, w_self, out_feat, grad_pre, out, w_part, agg, room, out_sems
):
    blocks, width, hidden = grad_pre.shape
    devices, per_owner = got.shape[:2]
    agg[...] = jnp.zeros_like(agg)
    for i in range(devices):
        for j in range(per_owner):
            agg[ids[i * per_owner + j]] += got[i, j].astype(F32)
    mine = feat[...].reshape(blocks * width, hidden)
    preact = jnp.dot(mine, w_self[...], preferred_element_type=F32)
    preact = preact + agg[...].reshape(blocks * width, hidden)
    sig = jax.nn.sigmoid(preact)
    grad = cot[...].reshape(blocks * width, hidden).astype(F32)
    grad = (grad * sig * (1.0 + preact * (1.0 - sig))).astype(BF16)
    grad_pre[...] = grad.reshape(blocks, width, hidden)
    copies = []
    size = devices // out_sems.shape[0]
    for p in range(out_sems.shape[0]):
        for i in range(p * size, (p + 1) * size):
            for j in range(per_owner):
                room[i, j] = grad_pre[ids[i * per_owner + j]]
        copies.append(send_out(room, out, out_sems, p, size))
    out_feat[...] = (preact * sig).astype(BF16).reshape(blocks, width, hidden)
    w_part[...] = lax.dot_general(
        mine, grad, (((0,), (0,)), ((), ())), preferred_element_type=F32
    )
    for copy in copies:
        copy.wait()


def backward_kernel(
    group, live, src, dst, got, raw, adj, out, w_part, turned, acc, held, room, sems, out_sems
):
    slots, block, hidden = raw.shape
    devices, per_owner, width = got.shape[:3]
    planes = block // width
    out_slots = out.shape[1]

    def term(k):
        return jnp.dot(turned[dst[k]], held[k], preferred_element_type=F32)

    def put(k, alive, value):
        acc[jnp.where(alive, src[k], slots)] += value

    start, run = edge_loop(group, live[0], adj, held, sems, term, put)
    start()
    for p in range(devices // planes):
        for j in range(per_owner):
            whole = jnp.concatenate([got[p * planes + q, j] for q in range(planes)], 0)
            turned[p * per_owner + j] = whole.T
    acc[...] = jnp.zeros_like(acc)
    run()
    copies = []
    for p in range(devices // planes):
        for j in range(out_slots):
            back = acc[p * out_slots + j].T.astype(BF16)
            for q in range(planes):
                room[p * planes + q, j] = back[q * width : (q + 1) * width]
        copies.append(send_out(room, out, out_sems, p, planes))
    total = jnp.zeros((hidden, hidden), F32)
    for s in range(slots):
        total += jnp.dot(acc[s].astype(BF16), raw[s], preferred_element_type=F32)
    w_part[...] = total.T
    for copy in copies:
        copy.wait()


def last_kernel(ids, got, grad_pre, w_self, w_msg, out, agg):
    blocks, width, hidden = grad_pre.shape
    devices, per_owner = got.shape[:2]
    agg[...] = jnp.zeros_like(agg)
    for i in range(devices):
        for j in range(per_owner):
            agg[ids[i * per_owner + j]] += got[i, j].astype(F32)
    grad_msg = agg[...].reshape(blocks * width, hidden).astype(BF16)
    turn = (((1,), (1,)), ((), ()))
    total = lax.dot_general(
        grad_pre[...].reshape(blocks * width, hidden),
        w_self[...],
        turn,
        preferred_element_type=F32,
    ) + lax.dot_general(grad_msg, w_msg[...], turn, preferred_element_type=F32)
    out[...] = total.astype(BF16).reshape(blocks, width, hidden)


def shape(dims, dtype):
    return jax.ShapeDtypeStruct(dims, dtype)


def in_hbm(x):
    return pltpu.with_memory_space_constraint(x, pltpu.HBM)


def body(
    node_feat, cotangent, w_msg, w_self, adjacency, edge_src, edge_dst, send_src, recv_dst, live
):
    block = adjacency.shape[-1]
    hidden = node_feat.shape[1]
    blocks = node_feat.shape[0] // block
    peers = lax.axis_size("edge")
    planes = lax.axis_size("feat")
    devices = peers * planes
    width = block // planes
    n_send = send_src.shape[-1]
    n_recv = recv_dst.shape[-1]
    adj = in_hbm(adjacency.reshape(-1, block, block))
    src = edge_src.reshape(-1)
    dst = edge_dst.reshape(-1)
    count = live.reshape(1)
    group = math.gcd(4, adj.shape[0])
    me = lax.axis_index("feat").reshape(1).astype(jnp.int32)
    params = pltpu.CompilerParams(vmem_limit_bytes=32 * 2**20)
    stages = stages_of(devices)

    ids = jnp.concatenate([send_src.reshape(peers, n_send), recv_dst.reshape(peers, n_recv)], 1)
    ids = gather_feat(ids).transpose(1, 0, 2)
    send_all = ids[:, :, :n_send].reshape(-1)
    recv_all = ids[:, :, n_send:].reshape(-1)

    wide_feat = in_hbm(node_feat.reshape(blocks, planes, width, hidden))
    wide_cot = in_hbm(cotangent.reshape(blocks, planes, width, hidden))
    square = pltpu.VMEM((hidden, hidden), BF16)
    sum_part = pltpu.VMEM((hidden, hidden), F32)
    quarter = pltpu.VMEM((blocks, width, hidden), BF16)
    rows_out = (peers * n_send, block, hidden)
    recv_out = (devices, n_recv, width, hidden)
    send_out_dims = (devices, n_send, width, hidden)
    out_sems = pltpu.SemaphoreType.DMA((peers,))
    outgoing, w_msg, w_self = pl.pallas_call(
        pick_kernel,
        out_shape=(pltpu.HBM(rows_out, BF16), square, square),
        in_specs=[SMEM] + [HBM] * 3,
        out_specs=(HBM, VMEM, VMEM),
        scratch_shapes=[
            pltpu.VMEM(rows_out, BF16),
            pltpu.SemaphoreType.DMA((peers * n_send + 2,)),
            pltpu.SemaphoreType.DMA((peers * n_send,)),
        ],
        compiler_params=params,
        name="pick_rows",
    )(
        send_src.transpose(0, 1, 3, 2).reshape(n_send, peers),
        in_hbm(node_feat.reshape(blocks, block, hidden)),
        in_hbm(w_msg),
        in_hbm(w_self),
    )
    raw = lax.all_to_all(outgoing, "edge", 0, 0, tiled=True)

    edge_room = pltpu.VMEM(adj.shape, BF16)
    edge_sems = pltpu.SemaphoreType.DMA((math.gcd(4, adj.shape[0] // group),))
    partials, feat_part, cot_part = pl.pallas_call(
        functools.partial(forward_kernel, group),
        out_shape=(pltpu.HBM(recv_out, BF16), quarter, quarter),
        in_specs=[SMEM] * 4 + [VMEM] * 2 + [HBM] * 3,
        out_specs=(HBM, VMEM, VMEM),
        scratch_shapes=[
            pltpu.VMEM((peers * n_send, block, hidden), BF16),
            pltpu.VMEM((peers * n_recv + 1, block, hidden), F32),
            edge_room,
            pltpu.VMEM(recv_out, BF16),
            edge_sems,
            pltpu.SemaphoreType.DMA((2,)),
            out_sems,
        ],
        compiler_params=params,
        name="edge_forward",
    )(count, me, src, dst, raw, w_msg, adj, wide_feat, wide_cot)
    got = lax.all_to_all(partials, BOTH, 0, 0, tiled=True)

    out_part, grad_pre, grad_out, wself_part = pl.pallas_call(
        owner_kernel,
        out_shape=(quarter, quarter, pltpu.HBM(recv_out, BF16), sum_part),
        in_specs=[SMEM] + [VMEM] * 4,
        out_specs=(VMEM, VMEM, HBM, VMEM),
        scratch_shapes=[
            pltpu.VMEM((blocks, width, hidden), F32),
            pltpu.VMEM(recv_out, BF16),
            out_sems,
        ],
        compiler_params=params,
        name="owner_dense",
    )(recv_all, got, feat_part, cot_part, w_self)
    grad_in = lax.all_to_all(grad_out, BOTH, 0, 0, tiled=True)
    (out_feat,) = join_feat(out_part, me, params)
    wself_part = split_core(wself_part, me)
    for bits in stages[1:2]:
        wself_part = sum_stage(wself_part, bits)
    grad_in, out_feat, wself_part = lax.optimization_barrier((grad_in, out_feat, wself_part))

    grad_partials, wmsg_part = pl.pallas_call(
        functools.partial(backward_kernel, group),
        out_shape=(pltpu.HBM(send_out_dims, BF16), sum_part),
        in_specs=[SMEM] * 3 + [VMEM] * 2 + [HBM],
        out_specs=(HBM, VMEM),
        scratch_shapes=[
            pltpu.VMEM((peers * n_recv, hidden, block), BF16),
            pltpu.VMEM((peers * n_send + 1, hidden, block), F32),
            edge_room,
            pltpu.VMEM(send_out_dims, BF16),
            edge_sems,
            out_sems,
        ],
        compiler_params=params,
        name="edge_backward",
    )(count, src, dst, grad_in, raw, adj)
    grad_partials, wmsg_part, wself_part = lax.optimization_barrier(
        (grad_partials, wmsg_part, wself_part)
    )
    grad_back = lax.all_to_all(grad_partials, BOTH, 0, 0, tiled=True)
    wmsg_part = split_core(wmsg_part, me)
    for bits in stages[1:2]:
        wmsg_part = sum_stage(wmsg_part, bits)
    sums = jnp.concatenate([wself_part, wmsg_part], 0)
    for bits in stages[2:]:
        sums = sum_stage(sums.astype(BF16), bits)
    grad_back, sums = lax.optimization_barrier((grad_back, sums))

    grad_part = pl.pallas_call(
        last_kernel,
        out_shape=pltpu.VMEM((blocks, width, hidden), BF16),
        in_specs=[SMEM] + [VMEM] * 4,
        out_specs=VMEM,
        scratch_shapes=[pltpu.VMEM((blocks, width, hidden), F32)],
        compiler_params=params,
        name="owner_last",
    )(send_all, grad_back, grad_pre, w_self, w_msg)
    grad_part, sums = lax.optimization_barrier((grad_part, sums))
    grad_feat, grad_wself, grad_wmsg = join_feat(grad_part, me, params, sums)
    return (out_feat, grad_feat, grad_wmsg, grad_wself)


def solution(mesh):
    in_specs = (
        P("edge", None),
        P("edge", None),
        P(),
        P(),
        P("edge", "feat", None, None, None),
        P("edge", "feat", None),
        P("edge", "feat", None),
        P("edge", "feat", None, None),
        P("edge", "feat", None, None),
        P("edge", "feat"),
    )
    out_specs = (P("edge", None), P("edge", None), P(), P())
    return jax.shard_map(body, mesh=mesh, in_specs=in_specs, out_specs=out_specs, check_vma=False)
```

```python
import functools
import math

import jax
import jax.numpy as jnp
from jax import lax
from jax.experimental import pallas as pl
from jax.experimental.pallas import tpu as pltpu
from jax.sharding import PartitionSpec as P

BOTH = ("edge", "feat")
F32 = jnp.float32
BF16 = jnp.bfloat16
VMEM = pl.BlockSpec(memory_space=pltpu.VMEM)
SMEM = pl.BlockSpec(memory_space=pltpu.SMEM)
HBM = pl.BlockSpec(memory_space=pltpu.HBM)
ANY = pl.BlockSpec(memory_space=pl.ANY)


def is_pow2(n):
    return n & (n - 1) == 0


def swap(x, axis, bit):
    size = lax.axis_size(axis)
    return lax.ppermute(x, axis, [(j, j ^ bit) for j in range(size)])


def gather_feat(x):
    size = lax.axis_size("feat")
    if not is_pow2(size):
        return lax.all_gather(x, "feat", axis=0)
    me = lax.axis_index("feat")
    held = x[None]
    bit = 1
    while bit < size:
        other = swap(held, "feat", bit)
        mine_low = (me & bit) == 0
        held = jnp.where(
            mine_low, jnp.concatenate([held, other], 0), jnp.concatenate([other, held], 0)
        )
        bit *= 2
    return held


def pieces_feat(x, beside=None):
    top = lax.axis_size("feat") // 2
    low = [1 << n for n in range(top.bit_length() - 1)][::-1]

    def spread(base, value):
        held = {base: value}
        for bit in low:
            held.update({m | bit: swap(v, "feat", bit) for m, v in list(held.items())})
        return held

    far = swap(x, "feat", top) if top else None
    held, other = spread(0, x), None
    if beside is not None:
        far, beside = lax.optimization_barrier((far, beside))
        other = swap_all(beside, 1)
    if top:
        held.update(spread(top, far))
    return [held[m] for m in sorted(held)], beside, other


def join_kernel(planes, count, me, *refs):
    pieces, refs = refs[: planes * count], refs[planes * count :]
    halves, (*outs, sems) = ((), refs) if len(refs) == count + 1 else (refs[:2], refs[2:])
    copies = [
        (part, outs[n // planes].at[:, me[0] ^ n % planes]) for n, part in enumerate(pieces)
    ]
    for n, total in enumerate(outs[count:]):
        rows = total.shape[1]
        copies += [
            (half.at[n * rows : (n + 1) * rows], total.at[(me[0] & 1) ^ m])
            for m, half in enumerate(halves)
        ]
    copies = [pltpu.make_async_copy(a, b, sems.at[n]) for n, (a, b) in enumerate(copies)]
    for copy in copies:
        copy.start()
    for copy in copies:
        copy.wait()


def join_feat(groups, halves, me, params):
    blocks, width, hidden = groups[0][0].shape
    planes = lax.axis_size("feat")
    count = 2 * halves[0].shape[0] // hidden if halves else 0
    out_shape = [pltpu.HBM((blocks, planes, width, hidden), BF16)] * len(groups)
    out_shape += [pltpu.HBM((2, hidden // 2, hidden), F32)] * count
    pieces = [piece for group in groups for piece in group]
    joined = pl.pallas_call(
        functools.partial(join_kernel, planes, len(groups)),
        out_shape=out_shape,
        in_specs=[SMEM] + [VMEM] * (len(pieces) + len(halves)),
        out_specs=[HBM] * len(out_shape),
        scratch_shapes=[pltpu.SemaphoreType.DMA((len(pieces) + 2 * count,))],
        compiler_params=params,
        name="join_rows",
    )(me, *pieces, *halves)
    return [v.reshape(-1, hidden) for v in joined]


def stages_of(count):
    bits = [1 << n for n in range(count.bit_length() - 1)]
    return [bits[:1]] + [bits[n : n + 2] for n in range(1, len(bits), 2)]


def swap_all(x, mask):
    count = lax.axis_size(BOTH)
    return lax.ppermute(x, BOTH, [(j, j ^ mask) for j in range(count)])


def sum_stage(x, bits):
    terms = {0: x}
    for bit in bits:
        terms.update({m | bit: swap_all(x, m | bit) for m in list(terms)})
    held = [terms[m].astype(F32) for m in sorted(terms)]
    while len(held) > 1:
        held = [held[n] + held[n + 1] for n in range(0, len(held), 2)]
    return held[0]


def split_core(x, me):
    halves = x.reshape(2, -1, x.shape[-1])
    low = (me & 1) == 0
    mine = jnp.where(low, halves[0], halves[1])
    other = jnp.where(low, halves[1], halves[0])
    return mine + swap_all(other, 1)


def pick_kernel(me, ids, rows, w_msg, w_self, *refs):
    n_send, peers = ids.shape
    *outs, w_msg_out, w_self_out, room, sems, out_sems = refs
    near = outs[0].shape[0] // n_send
    first = me[0] // near * near
    order = [me[0] ^ m for m in range(near, peers)] + [first + i for i in range(near)]
    places = [(outs[1 + m], 0) for m in range(peers - near)]
    places += [(outs[0], i * n_send) for i in range(near)]
    slots = [(n, j) for n in range(peers) for j in range(n_send)]
    ins = [
        pltpu.make_async_copy(
            rows.at[ids[j, order[n]]], room.at[n * n_send + j], sems.at[n * n_send + j]
        )
        for n, j in slots
    ]
    others = [
        pltpu.make_async_copy(w_msg, w_msg_out, sems.at[len(slots)]),
        pltpu.make_async_copy(w_self, w_self_out, sems.at[len(slots) + 1]),
    ]
    copies = [
        pltpu.make_async_copy(
            room.at[n * n_send + j],
            places[n][0].at[places[n][1] + j],
            out_sems.at[n * n_send + j],
        )
        for n, j in slots
    ]
    for copy in ins + others:
        copy.start()
    for one, two in zip(ins, copies):
        one.wait()
        two.start()
    for copy in others + copies:
        copy.wait()


def pieces_of(me, raw):
    near, *far = raw
    per_owner = far[0].shape[0] if far else near.shape[0]
    owners = near.shape[0] // per_owner
    yield me // owners * owners * per_owner, near
    for m, rows in enumerate(far):
        yield (me ^ (owners + m)) * per_owner, rows


def fetch_kernel(me, *refs):
    *ins, out, sems = refs
    copies = [
        pltpu.make_async_copy(
            a if me is None else a.at[:, me[0]], out if me is None else out.at[n], sems.at[n]
        )
        for n, a in enumerate(ins)
    ]
    for copy in copies:
        copy.start()
    for copy in copies:
        copy.wait()


def fetch(me, arrays, dims, params, name):
    kernel, specs, args = fetch_kernel, [SMEM], [me]
    if me is None:
        kernel, specs, args = functools.partial(fetch_kernel, None), [], []
    return pl.pallas_call(
        kernel,
        out_shape=pltpu.VMEM(dims, BF16),
        in_specs=specs + [HBM] * len(arrays),
        out_specs=VMEM,
        scratch_shapes=[pltpu.SemaphoreType.DMA((len(arrays),))],
        compiler_params=params,
        cost_estimate=pl.CostEstimate(
            flops=0, bytes_accessed=4 * math.prod(dims), transcendentals=0
        ),
        name=name,
    )(*args, *arrays)


def edge_loop(group, count, term, put):
    def step(turn, carry):
        ks = [turn * group + u for u in range(group)]
        terms = [term(k) for k in ks]
        for k, value in zip(ks, terms):
            put(k, k < count, value)
        return carry

    lax.fori_loop(0, (count + group - 1) // group, step, 0)


def copy_ids(pairs, sems):
    copies = [pltpu.make_async_copy(a, b, sems.at[n]) for n, (a, b) in enumerate(pairs)]
    for copy in copies:
        copy.start()
    return copies


def send_out(room, out, sems, p, size):
    copy = pltpu.make_async_copy(
        room.at[p * size : (p + 1) * size], out.at[p * size : (p + 1) * size], sems.at[p]
    )
    copy.start()
    return copy


def forward_kernel(
    group, live, me, src_in, dst_in, w_msg, adj, *refs
):
    *raw, out, msgs, acc, room, src, dst, sems, out_sems = refs
    slots, block, hidden = msgs.shape
    per_owner, width = out.shape[1:3]
    planes = block // width
    ids = copy_ids([(src_in, src), (dst_in, dst)], sems)
    for first, rows in pieces_of(me[0], raw):
        flat = rows[...].reshape(-1, hidden)
        piece = jnp.dot(flat, w_msg[...], preferred_element_type=F32).astype(BF16)
        msgs[pl.ds(first, rows.shape[0])] = piece.reshape(rows.shape)
    acc[...] = jnp.zeros_like(acc)
    for copy in ids:
        copy.wait()

    def term(k):
        return jnp.dot(adj[k], msgs[src[k]], preferred_element_type=F32)

    def put(k, alive, value):
        acc[jnp.where(alive, dst[k], slots)] += value

    edge_loop(group, live[0], term, put)
    copies = []
    for p in range(out.shape[0] // planes):
        for j in range(per_owner):
            for q in range(planes):
                room[p * planes + q, j] = acc[
                    p * per_owner + j, q * width : (q + 1) * width
                ].astype(BF16)
        copies.append(send_out(room, out, out_sems, p, planes))
    for copy in copies:
        copy.wait()


def owner_kernel(
    ids, got, rows, w_self, out_feat, grad_pre, out, w_part, agg, held, room, out_room, out_sems
):
    blocks, width, hidden = held.shape
    devices, per_owner = got.shape[:2]
    agg[...] = jnp.zeros_like(agg)
    for i in range(devices):
        for j in range(per_owner):
            agg[ids[i * per_owner + j]] += got[i, j].astype(F32)
    mine = rows[0].reshape(blocks * width, hidden)
    preact = jnp.dot(mine, w_self[...], preferred_element_type=F32)
    preact = preact + agg[...].reshape(blocks * width, hidden)
    sig = jax.nn.sigmoid(preact)
    grad = rows[1].reshape(blocks * width, hidden).astype(F32)
    grad = (grad * sig * (1.0 + preact * (1.0 - sig))).astype(BF16)
    held[...] = grad.reshape(blocks, width, hidden)
    copies = []
    peers = out_sems.shape[0] - 2
    size = devices // peers
    for p in range(peers):
        for i in range(p * size, (p + 1) * size):
            for j in range(per_owner):
                room[i, j] = held[ids[i * per_owner + j]]
        copies.append(send_out(room, out, out_sems, p, size))
    out_room[...] = (preact * sig).astype(BF16).reshape(blocks, width, hidden)
    for n, (a, b) in enumerate([(out_room, out_feat), (held, grad_pre)]):
        copies.append(pltpu.make_async_copy(a, b, out_sems.at[peers + n]))
        copies[-1].start()
    w_part[...] = lax.dot_general(
        mine, grad, (((0,), (0,)), ((), ())), preferred_element_type=F32
    )
    for copy in copies:
        copy.wait()


def backward_kernel(group, live, me, src_in, dst_in, got, adj, *refs):
    *raw, out, w_part, turned, acc, room, src, dst, sems, out_sems = refs
    slots, hidden, block = acc.shape
    slots -= 1
    devices, per_owner, width = got.shape[:3]
    planes = block // width
    out_slots = out.shape[1]
    ids = copy_ids([(src_in, src), (dst_in, dst)], sems)
    for p in range(devices // planes):
        for j in range(per_owner):
            whole = jnp.concatenate([got[p * planes + q, j] for q in range(planes)], 0)
            turned[p * per_owner + j] = whole.T
    acc[...] = jnp.zeros_like(acc)
    for copy in ids:
        copy.wait()

    def term(k):
        return jnp.dot(turned[dst[k]], adj[k], preferred_element_type=F32)

    def put(k, alive, value):
        acc[jnp.where(alive, src[k], slots)] += value

    edge_loop(group, live[0], term, put)
    copies = []
    for p in range(devices // planes):
        for j in range(out_slots):
            back = acc[p * out_slots + j].T.astype(BF16)
            for q in range(planes):
                room[p * planes + q, j] = back[q * width : (q + 1) * width]
        copies.append(send_out(room, out, out_sems, p, planes))
    total = jnp.zeros((hidden, hidden), F32)
    for first, rows in pieces_of(me[0], raw):
        for s in range(rows.shape[0]):
            total += jnp.dot(acc[first + s].astype(BF16), rows[s], preferred_element_type=F32)
    w_part[...] = total.T
    for copy in copies:
        copy.wait()


def last_kernel(ids, got, grad_pre, w_self, w_msg, out, agg):
    blocks, width, hidden = grad_pre.shape
    devices, per_owner = got.shape[:2]
    agg[...] = jnp.zeros_like(agg)
    for i in range(devices):
        for j in range(per_owner):
            agg[ids[i * per_owner + j]] += got[i, j].astype(F32)
    grad_msg = agg[...].reshape(blocks * width, hidden).astype(BF16)
    turn = (((1,), (1,)), ((), ()))
    total = lax.dot_general(
        grad_pre[...].reshape(blocks * width, hidden),
        w_self[...],
        turn,
        preferred_element_type=F32,
    ) + lax.dot_general(grad_msg, w_msg[...], turn, preferred_element_type=F32)
    out[...] = total.astype(BF16).reshape(blocks, width, hidden)


def shape(dims, dtype):
    return jax.ShapeDtypeStruct(dims, dtype)


def in_hbm(x):
    return pltpu.with_memory_space_constraint(x, pltpu.HBM)


def body(
    node_feat, cotangent, w_msg, w_self, adjacency, edge_src, edge_dst, send_src, recv_dst, live
):
    block = adjacency.shape[-1]
    hidden = node_feat.shape[1]
    blocks = node_feat.shape[0] // block
    peers = lax.axis_size("edge")
    planes = lax.axis_size("feat")
    devices = peers * planes
    width = block // planes
    n_send = send_src.shape[-1]
    n_recv = recv_dst.shape[-1]
    adj = in_hbm(adjacency.reshape(-1, block, block))
    src = in_hbm(edge_src.reshape(-1))
    dst = in_hbm(edge_dst.reshape(-1))
    count = live.reshape(1)
    group = math.gcd(16, adj.shape[0])
    me = lax.axis_index("feat").reshape(1).astype(jnp.int32)
    params = pltpu.CompilerParams(vmem_limit_bytes=32 * 2**20)
    stages = stages_of(devices)

    ids = jnp.concatenate([send_src.reshape(peers, n_send), recv_dst.reshape(peers, n_recv)], 1)
    ids = gather_feat(ids).transpose(1, 0, 2)
    send_all = ids[:, :, :n_send].reshape(-1)
    recv_all = ids[:, :, n_send:].reshape(-1)

    wide_feat = in_hbm(node_feat.reshape(blocks, planes, width, hidden))
    wide_cot = in_hbm(cotangent.reshape(blocks, planes, width, hidden))
    square = pltpu.VMEM((hidden, hidden), BF16)
    sum_part = pltpu.VMEM((hidden, hidden), F32)
    rows_out = (peers * n_send, block, hidden)
    recv_out = (devices, n_recv, width, hidden)
    send_out_dims = (devices, n_send, width, hidden)
    out_sems = pltpu.SemaphoreType.DMA((peers,))
    here = lax.axis_index("edge").reshape(1).astype(jnp.int32)
    near = peers // 2 if is_pow2(peers) and 1 < peers <= 16 else peers
    few = (n_send, block, hidden)
    *outgoing, w_msg, w_self = pl.pallas_call(
        pick_kernel,
        out_shape=[pltpu.HBM((near * n_send, block, hidden), BF16)]
        + [pltpu.HBM(few, BF16)] * (peers - near)
        + [square, square],
        in_specs=[SMEM] * 2 + [HBM] * 3,
        out_specs=[HBM] * (peers - near + 1) + [VMEM, VMEM],
        scratch_shapes=[
            pltpu.VMEM(rows_out, BF16),
            pltpu.SemaphoreType.DMA((peers * n_send + 2,)),
            pltpu.SemaphoreType.DMA((peers * n_send,)),
        ],
        compiler_params=params,
        name="pick_rows",
    )(
        here,
        in_hbm(send_src.transpose(0, 1, 3, 2).reshape(n_send, peers)),
        in_hbm(node_feat.reshape(blocks, block, hidden)),
        in_hbm(w_msg),
        in_hbm(w_self),
    )
    raw = [swap(rows, "edge", near + m) for m, rows in enumerate(outgoing[1:])]
    groups = [list(range(g, g + near)) for g in range(0, peers, near)]
    raw = [
        lax.all_to_all(outgoing[0], "edge", 0, 0, tiled=True, axis_index_groups=groups)
    ] + raw

    adj = fetch(None, [adj], adj.shape, params, "fetch_edges")
    ids_room = [pltpu.SMEM(src.shape, src.dtype)] * 2 + [pltpu.SemaphoreType.DMA((2,))]
    partials = pl.pallas_call(
        functools.partial(forward_kernel, group),
        out_shape=pltpu.HBM(recv_out, BF16),
        in_specs=[SMEM] * 2 + [HBM] * 2 + [VMEM] * (2 + len(raw)),
        out_specs=HBM,
        scratch_shapes=[
            pltpu.VMEM((peers * n_send, block, hidden), BF16),
            pltpu.VMEM((peers * n_recv + 1, block, hidden), F32),
            pltpu.VMEM(recv_out, BF16),
            *ids_room,
            out_sems,
        ],
        compiler_params=params,
        name="edge_forward",
    )(count, here, src, dst, w_msg, adj, *raw)
    later, partials = lax.optimization_barrier((me, partials))
    got = lax.all_to_all(partials, BOTH, 0, 0, tiled=True)
    rows = fetch(later, [wide_feat, wide_cot], (2, blocks, width, hidden), params, "fetch_rows")

    out_part, grad_pre, grad_out, wself_part = pl.pallas_call(
        owner_kernel,
        out_shape=(
            pltpu.HBM((blocks, width, hidden), BF16),
            pltpu.HBM((blocks, width, hidden), BF16),
            pltpu.HBM(recv_out, BF16),
            sum_part,
        ),
        in_specs=[SMEM] + [VMEM] * 3,
        out_specs=(HBM, HBM, HBM, VMEM),
        scratch_shapes=[
            pltpu.VMEM((blocks, width, hidden), F32),
            pltpu.VMEM((blocks, width, hidden), BF16),
            pltpu.VMEM(recv_out, BF16),
            pltpu.VMEM((blocks, width, hidden), BF16),
            pltpu.SemaphoreType.DMA((peers + 2,)),
        ],
        compiler_params=params,
        name="owner_dense",
    )(recv_all, got, rows, w_self)
    grad_in = lax.all_to_all(grad_out, BOTH, 0, 0, tiled=True)
    out_pieces, _, _ = pieces_feat(out_part)
    (out_feat,) = join_feat([out_pieces], [], me, params)
    wself_part = split_core(wself_part, me)
    for bits in stages[1:2]:
        wself_part = sum_stage(wself_part, bits)
    grad_in, out_feat, wself_part = lax.optimization_barrier((grad_in, out_feat, wself_part))

    grad_partials, wmsg_part = pl.pallas_call(
        functools.partial(backward_kernel, group),
        out_shape=(pltpu.HBM(send_out_dims, BF16), sum_part),
        in_specs=[SMEM] * 2 + [HBM] * 2 + [VMEM] * (2 + len(raw)),
        out_specs=(HBM, VMEM),
        scratch_shapes=[
            pltpu.VMEM((peers * n_recv, hidden, block), BF16),
            pltpu.VMEM((peers * n_send + 1, hidden, block), F32),
            pltpu.VMEM(send_out_dims, BF16),
            *ids_room,
            out_sems,
        ],
        compiler_params=params,
        name="edge_backward",
    )(count, here, src, dst, grad_in, adj, *raw)
    grad_partials, wmsg_part, wself_part = lax.optimization_barrier(
        (grad_partials, wmsg_part, wself_part)
    )
    grad_back = lax.all_to_all(grad_partials, BOTH, 0, 0, tiled=True)
    wmsg_part = split_core(wmsg_part, me)
    for bits in stages[1:2]:
        wmsg_part = sum_stage(wmsg_part, bits)
    sums = jnp.concatenate([wself_part, wmsg_part], 0)
    for bits in stages[2:]:
        sums = sum_stage(sums.astype(BF16), bits)

    grad_part = pl.pallas_call(
        last_kernel,
        out_shape=pltpu.VMEM((blocks, width, hidden), BF16),
        in_specs=[SMEM] + [VMEM] * 4,
        out_specs=VMEM,
        scratch_shapes=[pltpu.VMEM((blocks, width, hidden), F32)],
        compiler_params=params,
        name="owner_last",
    )(send_all, grad_back, grad_pre, w_self, w_msg)
    grad_pieces, sums, other = pieces_feat(grad_part, sums)
    grad_feat, grad_wself, grad_wmsg = join_feat([grad_pieces], [sums, other], me, params)
    return (out_feat, grad_feat, grad_wmsg, grad_wself)


def solution(mesh):
    in_specs = (
        P("edge", None),
        P("edge", None),
        P(),
        P(),
        P("edge", "feat", None, None, None),
        P("edge", "feat", None),
        P("edge", "feat", None),
        P("edge", "feat", None, None),
        P("edge", "feat", None, None),
        P("edge", "feat"),
    )
    out_specs = (P("edge", None), P("edge", None), P(), P())
    return jax.shard_map(body, mesh=mesh, in_specs=in_specs, out_specs=out_specs, check_vma=False)
```

```python
import functools
import math

import jax
import jax.numpy as jnp
from jax import lax
from jax.experimental import pallas as pl
from jax.experimental.pallas import tpu as pltpu
from jax.sharding import PartitionSpec as P

BOTH = ("edge", "feat")
F32 = jnp.float32
BF16 = jnp.bfloat16
VMEM = pl.BlockSpec(memory_space=pltpu.VMEM)
SMEM = pl.BlockSpec(memory_space=pltpu.SMEM)
HBM = pl.BlockSpec(memory_space=pltpu.HBM)
ANY = pl.BlockSpec(memory_space=pl.ANY)


def is_pow2(n):
    return n & (n - 1) == 0


def swap(x, axis, bit):
    size = lax.axis_size(axis)
    return lax.ppermute(x, axis, [(j, j ^ bit) for j in range(size)])


def gather_feat(x):
    size = lax.axis_size("feat")
    if not is_pow2(size):
        return lax.all_gather(x, "feat", axis=0)
    me = lax.axis_index("feat")
    held = x[None]
    bit = 1
    while bit < size:
        other = swap(held, "feat", bit)
        mine_low = (me & bit) == 0
        held = jnp.where(
            mine_low, jnp.concatenate([held, other], 0), jnp.concatenate([other, held], 0)
        )
        bit *= 2
    return held


def pieces_feat(x, beside=None):
    top = lax.axis_size("feat") // 2
    low = [1 << n for n in range(top.bit_length() - 1)][::-1]

    def spread(base, value):
        held = {base: value}
        for bit in low:
            held.update({m | bit: swap(v, "feat", bit) for m, v in list(held.items())})
        return held

    far = swap(x, "feat", top) if top else None
    held, other = spread(0, x), None
    if beside is not None:
        far, beside = lax.optimization_barrier((far, beside))
        other = swap_all(beside, 1)
    if top:
        held.update(spread(top, far))
    return [held[m] for m in sorted(held)], beside, other


def join_kernel(planes, bounce, *refs):
    me = lax.axis_index("feat")
    pieces, refs = refs[:planes], refs[planes:]
    if bounce:
        out, room, sems, in_sems = refs
        ins = [
            pltpu.make_async_copy(piece, room.at[n], in_sems.at[n])
            for n, piece in enumerate(pieces)
        ]
        for copy in ins:
            copy.start()
        copies = [(room.at[n], out.at[:, me ^ n]) for n in range(planes)]
    else:
        ins = []
        halves, (out, *sums, sems) = refs[:2], refs[2:]
        copies = [(piece, out.at[:, me ^ n]) for n, piece in enumerate(pieces)]
        for n, total in enumerate(sums):
            rows = total.shape[1]
            copies += [
                (half.at[n * rows : (n + 1) * rows], total.at[(me & 1) ^ m])
                for m, half in enumerate(halves)
            ]
    copies = [pltpu.make_async_copy(a, b, sems.at[n]) for n, (a, b) in enumerate(copies)]
    for n, copy in enumerate(copies):
        if bounce:
            ins[n].wait()
        copy.start()
    for copy in copies:
        copy.wait()


def join_feat(pieces, halves, params):
    blocks, width, hidden = pieces[0].shape
    planes = len(pieces)
    count = 2 * halves[0].shape[0] // hidden if halves else 0
    out_shape = [pltpu.HBM((blocks, planes, width, hidden), BF16)]
    out_shape += [pltpu.HBM((2, hidden // 2, hidden), F32)] * count
    scratch = [pltpu.SemaphoreType.DMA((planes + 2 * count,))]
    if not halves:
        pieces = [in_hbm(piece) for piece in pieces]
        scratch = [pltpu.VMEM((planes, blocks, width, hidden), BF16), *scratch * 2]
    joined = pl.pallas_call(
        functools.partial(join_kernel, planes, not halves),
        out_shape=out_shape,
        in_specs=[VMEM if halves else HBM] * planes + [VMEM] * len(halves),
        out_specs=[HBM] * len(out_shape),
        scratch_shapes=scratch,
        compiler_params=params,
        name="join_rows",
    )(*pieces, *halves)
    return [v.reshape(-1, hidden) for v in joined]


def stages_of(count):
    bits = [1 << n for n in range(count.bit_length() - 1)]
    return [bits[:1]] + [bits[n : n + 2] for n in range(1, len(bits), 2)]


def swap_all(x, mask):
    count = lax.axis_size(BOTH)
    return lax.ppermute(x, BOTH, [(j, j ^ mask) for j in range(count)])


def sum_stage(x, bits):
    terms = {0: x}
    for bit in bits:
        terms.update({m | bit: swap_all(x, m | bit) for m in list(terms)})
    held = [terms[m].astype(F32) for m in sorted(terms)]
    while len(held) > 1:
        held = [held[n] + held[n + 1] for n in range(0, len(held), 2)]
    return held[0]


def split_core(x, me):
    halves = x.reshape(2, -1, x.shape[-1])
    low = (me & 1) == 0
    mine = jnp.where(low, halves[0], halves[1])
    other = jnp.where(low, halves[1], halves[0])
    return mine + swap_all(other, 1)


def pick_kernel(masks, ids, rows, w_msg, w_self, *refs):
    n_send, peers = ids.shape
    *outs, w_msg_out, w_self_out, room, sems, out_sems = refs
    me = lax.axis_index("edge")
    slots = [(n, j) for n in range(peers) for j in range(n_send)]
    ins = [
        pltpu.make_async_copy(
            rows.at[ids[j, me ^ masks[n]]], room.at[n * n_send + j], sems.at[n * n_send + j]
        )
        for n, j in slots
    ]
    others = [
        pltpu.make_async_copy(w_msg, w_msg_out, sems.at[len(slots)]),
        pltpu.make_async_copy(w_self, w_self_out, sems.at[len(slots) + 1]),
    ]
    copies = [
        pltpu.make_async_copy(
            room.at[n * n_send + j],
            outs[n].at[j],
            out_sems.at[n * n_send + j],
        )
        for n, j in slots
    ]
    for copy in ins + others:
        copy.start()
    for one, two in zip(ins, copies):
        one.wait()
        two.start()
    for copy in others + copies:
        copy.wait()


def pieces_of(masks, raw):
    me = lax.axis_index("edge")
    return [((me ^ mask) * rows.shape[0], rows) for mask, rows in zip(masks, raw)]


def mask_order(peers):
    return sorted(range(peers), key=lambda m: (-m.bit_length(), -m))


def fetch_kernel(quarter, *refs):
    *ins, out, sems = refs
    me = lax.axis_index("feat")
    copies = [
        pltpu.make_async_copy(
            a.at[:, me] if quarter else a, out.at[n] if quarter else out, sems.at[n]
        )
        for n, a in enumerate(ins)
    ]
    for copy in copies:
        copy.start()
    for copy in copies:
        copy.wait()


def fetch(quarter, arrays, dims, params, name):
    return pl.pallas_call(
        functools.partial(fetch_kernel, quarter),
        out_shape=pltpu.VMEM(dims, BF16),
        in_specs=[HBM] * len(arrays),
        out_specs=VMEM,
        scratch_shapes=[pltpu.SemaphoreType.DMA((len(arrays),))],
        compiler_params=params,
        cost_estimate=pl.CostEstimate(
            flops=0, bytes_accessed=4 * math.prod(dims), transcendentals=0
        ),
        name=name,
    )(*arrays)


def edge_loop(group, count, term, put):
    def step(turn, carry):
        ks = [turn * group + u for u in range(group)]
        terms = [term(k) for k in ks]
        for k, value in zip(ks, terms):
            put(k, k < count, value)
        return carry

    lax.fori_loop(0, (count + group - 1) // group, step, 0)


def copy_ids(pairs, sems):
    copies = [pltpu.make_async_copy(a, b, sems.at[n]) for n, (a, b) in enumerate(pairs)]
    for copy in copies:
        copy.start()
    return copies


def send_out(room, out, sems, p, size):
    copy = pltpu.make_async_copy(
        room.at[p * size : (p + 1) * size], out.at[p * size : (p + 1) * size], sems.at[p]
    )
    copy.start()
    return copy


def forward_kernel(
    group, masks, live, src_in, dst_in, w_msg, adj, *refs
):
    *raw, out, msgs, acc, room, src, dst, sems, out_sems = refs
    slots, block, hidden = msgs.shape
    per_owner, width = out.shape[1:3]
    planes = block // width
    ids = copy_ids([(src_in, src), (dst_in, dst)], sems)
    for first, rows in pieces_of(masks, raw):
        flat = rows[...].reshape(-1, hidden)
        piece = jnp.dot(flat, w_msg[...], preferred_element_type=F32).astype(BF16)
        msgs[pl.ds(first, rows.shape[0])] = piece.reshape(rows.shape)
    acc[...] = jnp.zeros_like(acc)
    for copy in ids:
        copy.wait()

    def term(k):
        return jnp.dot(adj[k], msgs[src[k]], preferred_element_type=F32)

    def put(k, alive, value):
        acc[jnp.where(alive, dst[k], slots)] += value

    edge_loop(group, live[0], term, put)
    copies = []
    for p in range(out.shape[0] // planes):
        for j in range(per_owner):
            for q in range(planes):
                room[p * planes + q, j] = acc[
                    p * per_owner + j, q * width : (q + 1) * width
                ].astype(BF16)
        copies.append(send_out(room, out, out_sems, p, planes))
    for copy in copies:
        copy.wait()


def owner_kernel(
    ids, got, rows, w_self, out_feat, grad_pre, out, w_part, agg, held, room, out_room, out_sems
):
    blocks, width, hidden = held.shape
    devices, per_owner = got.shape[:2]
    agg[...] = jnp.zeros_like(agg)
    for i in range(devices):
        for j in range(per_owner):
            agg[ids[i * per_owner + j]] += got[i, j].astype(F32)
    mine = rows[0].reshape(blocks * width, hidden)
    preact = jnp.dot(mine, w_self[...], preferred_element_type=F32)
    preact = preact + agg[...].reshape(blocks * width, hidden)
    sig = jax.nn.sigmoid(preact)
    grad = rows[1].reshape(blocks * width, hidden).astype(F32)
    grad = (grad * sig * (1.0 + preact * (1.0 - sig))).astype(BF16)
    held[...] = grad.reshape(blocks, width, hidden)
    copies = []
    peers = out_sems.shape[0] - 2
    size = devices // peers
    for p in range(peers):
        for i in range(p * size, (p + 1) * size):
            for j in range(per_owner):
                room[i, j] = held[ids[i * per_owner + j]]
        copies.append(send_out(room, out, out_sems, p, size))
    out_room[...] = (preact * sig).astype(BF16).reshape(blocks, width, hidden)
    for n, (a, b) in enumerate([(out_room, out_feat), (held, grad_pre)]):
        copies.append(pltpu.make_async_copy(a, b, out_sems.at[peers + n]))
        copies[-1].start()
    w_part[...] = lax.dot_general(
        mine, grad, (((0,), (0,)), ((), ())), preferred_element_type=F32
    )
    for copy in copies:
        copy.wait()


def backward_kernel(group, masks, live, src_in, dst_in, got, adj, *refs):
    *raw, out, w_part, turned, acc, room, src, dst, sems, out_sems = refs
    slots, hidden, block = acc.shape
    slots -= 1
    devices, per_owner, width = got.shape[:3]
    planes = block // width
    out_slots = out.shape[1]
    ids = copy_ids([(src_in, src), (dst_in, dst)], sems)
    for p in range(devices // planes):
        for j in range(per_owner):
            whole = jnp.concatenate([got[p * planes + q, j] for q in range(planes)], 0)
            turned[p * per_owner + j] = whole.T
    acc[...] = jnp.zeros_like(acc)
    for copy in ids:
        copy.wait()

    def term(k):
        return jnp.dot(turned[dst[k]], adj[k], preferred_element_type=F32)

    def put(k, alive, value):
        acc[jnp.where(alive, src[k], slots)] += value

    edge_loop(group, live[0], term, put)
    copies = []
    for p in range(devices // planes):
        for j in range(out_slots):
            back = acc[p * out_slots + j].astype(BF16).T
            for q in range(planes):
                room[p * planes + q, j] = back[q * width : (q + 1) * width]
        copies.append(send_out(room, out, out_sems, p, planes))
    total = jnp.zeros((hidden, hidden), F32)
    for first, rows in pieces_of(masks, raw):
        for s in range(rows.shape[0]):
            total += jnp.dot(acc[first + s].astype(BF16), rows[s], preferred_element_type=F32)
    w_part[...] = total.T
    for copy in copies:
        copy.wait()


def last_kernel(ids, got, grad_pre, w_self, w_msg, out, agg):
    blocks, width, hidden = grad_pre.shape
    devices, per_owner = got.shape[:2]
    agg[...] = jnp.zeros_like(agg)
    for i in range(devices):
        for j in range(per_owner):
            agg[ids[i * per_owner + j]] += got[i, j].astype(F32)
    grad_msg = agg[...].reshape(blocks * width, hidden).astype(BF16)
    turn = (((1,), (1,)), ((), ()))
    total = lax.dot_general(
        grad_pre[...].reshape(blocks * width, hidden),
        w_self[...],
        turn,
        preferred_element_type=F32,
    ) + lax.dot_general(grad_msg, w_msg[...], turn, preferred_element_type=F32)
    out[...] = total.astype(BF16).reshape(blocks, width, hidden)


def shape(dims, dtype):
    return jax.ShapeDtypeStruct(dims, dtype)


def in_hbm(x):
    return pltpu.with_memory_space_constraint(x, pltpu.HBM)


def body(
    node_feat, cotangent, w_msg, w_self, adjacency, edge_src, edge_dst, send_src, recv_dst, live
):
    block = adjacency.shape[-1]
    hidden = node_feat.shape[1]
    blocks = node_feat.shape[0] // block
    peers = lax.axis_size("edge")
    planes = lax.axis_size("feat")
    devices = peers * planes
    width = block // planes
    n_send = send_src.shape[-1]
    n_recv = recv_dst.shape[-1]
    adj = in_hbm(adjacency.reshape(-1, block, block))
    src = in_hbm(edge_src.reshape(-1))
    dst = in_hbm(edge_dst.reshape(-1))
    count = live.reshape(1)
    group = math.gcd(16, adj.shape[0])
    me = lax.axis_index("feat").reshape(1).astype(jnp.int32)
    params = pltpu.CompilerParams(vmem_limit_bytes=32 * 2**20)
    stages = stages_of(devices)

    ids = jnp.concatenate([send_src.reshape(peers, n_send), recv_dst.reshape(peers, n_recv)], 1)
    ids = gather_feat(ids).transpose(1, 0, 2)
    send_all = ids[:, :, :n_send].reshape(-1)
    recv_all = ids[:, :, n_send:].reshape(-1)

    square = pltpu.VMEM((hidden, hidden), BF16)
    sum_part = pltpu.VMEM((hidden, hidden), F32)
    rows_out = (peers * n_send, block, hidden)
    recv_out = (devices, n_recv, width, hidden)
    send_out_dims = (devices, n_send, width, hidden)
    out_sems = pltpu.SemaphoreType.DMA((peers,))
    masks = mask_order(peers)
    few = (n_send, block, hidden)
    *outgoing, w_msg, w_self = pl.pallas_call(
        functools.partial(pick_kernel, masks),
        out_shape=[pltpu.HBM(few, BF16)] * peers + [square, square],
        in_specs=[SMEM] + [HBM] * 3,
        out_specs=[HBM] * peers + [VMEM, VMEM],
        scratch_shapes=[
            pltpu.VMEM(rows_out, BF16),
            pltpu.SemaphoreType.DMA((peers * n_send + 2,)),
            pltpu.SemaphoreType.DMA((peers * n_send,)),
        ],
        compiler_params=params,
        name="pick_rows",
    )(
        in_hbm(send_src.transpose(0, 1, 3, 2).reshape(n_send, peers)),
        in_hbm(node_feat.reshape(blocks, block, hidden)),
        in_hbm(w_msg),
        in_hbm(w_self),
    )
    raw = [swap(rows, "edge", mask) if mask else rows for mask, rows in zip(masks, outgoing)]

    adj = fetch(False, [adj], adj.shape, params, "fetch_edges")
    ids_room = [pltpu.SMEM(v.shape, v.dtype) for v in (src, dst)]
    ids_room.append(pltpu.SemaphoreType.DMA((2,)))
    partials = pl.pallas_call(
        functools.partial(forward_kernel, group, masks),
        out_shape=pltpu.HBM(recv_out, BF16),
        in_specs=[SMEM] + [HBM] * 2 + [VMEM] * (2 + len(raw)),
        out_specs=HBM,
        scratch_shapes=[
            pltpu.VMEM((peers * n_send, block, hidden), BF16),
            pltpu.VMEM((peers * n_recv + 1, block, hidden), F32),
            pltpu.VMEM(recv_out, BF16),
            *ids_room,
            out_sems,
        ],
        compiler_params=params,
        name="edge_forward",
    )(count, src, dst, w_msg, adj, *raw)
    wide_feat, wide_cot, partials = lax.optimization_barrier(
        (node_feat, cotangent, partials)
    )
    wide_feat = in_hbm(wide_feat.reshape(blocks, planes, width, hidden))
    wide_cot = in_hbm(wide_cot.reshape(blocks, planes, width, hidden))
    got = lax.all_to_all(partials, BOTH, 0, 0, tiled=True)
    rows = fetch(True, [wide_feat, wide_cot], (2, blocks, width, hidden), params, "fetch_rows")

    out_part, grad_pre, grad_out, wself_part = pl.pallas_call(
        owner_kernel,
        out_shape=(
            pltpu.HBM((blocks, width, hidden), BF16),
            pltpu.HBM((blocks, width, hidden), BF16),
            pltpu.HBM(recv_out, BF16),
            sum_part,
        ),
        in_specs=[SMEM] + [VMEM] * 3,
        out_specs=(HBM, HBM, HBM, VMEM),
        scratch_shapes=[
            pltpu.VMEM((blocks, width, hidden), F32),
            pltpu.VMEM((blocks, width, hidden), BF16),
            pltpu.VMEM(recv_out, BF16),
            pltpu.VMEM((blocks, width, hidden), BF16),
            pltpu.SemaphoreType.DMA((peers + 2,)),
        ],
        compiler_params=params,
        name="owner_dense",
    )(recv_all, got, rows, w_self)
    grad_in = lax.all_to_all(grad_out, BOTH, 0, 0, tiled=True)
    out_pieces, _, _ = pieces_feat(out_part)
    wself_part = split_core(wself_part, me)
    for bits in stages[1:2]:
        wself_part = sum_stage(wself_part, bits)
    grad_in, out_pieces, wself_part = lax.optimization_barrier(
        (grad_in, out_pieces, wself_part)
    )

    grad_partials, wmsg_part = pl.pallas_call(
        functools.partial(backward_kernel, group, masks),
        out_shape=(pltpu.HBM(send_out_dims, BF16), sum_part),
        in_specs=[SMEM] + [HBM] * 2 + [VMEM] * (2 + len(raw)),
        out_specs=(HBM, VMEM),
        scratch_shapes=[
            pltpu.VMEM((peers * n_recv, hidden, block), BF16),
            pltpu.VMEM((peers * n_send + 1, hidden, block), F32),
            pltpu.VMEM(send_out_dims, BF16),
            *ids_room,
            out_sems,
        ],
        compiler_params=params,
        name="edge_backward",
    )(count, src, dst, grad_in, adj, *raw)
    grad_partials, wmsg_part, wself_part, out_pieces = lax.optimization_barrier(
        (grad_partials, wmsg_part, wself_part, out_pieces)
    )
    (out_feat,) = join_feat(out_pieces, [], params)
    grad_back = lax.all_to_all(grad_partials, BOTH, 0, 0, tiled=True)
    wmsg_part = split_core(wmsg_part, me)
    for bits in stages[1:2]:
        wmsg_part = sum_stage(wmsg_part, bits)
    sums = jnp.concatenate([wself_part, wmsg_part], 0)
    for bits in stages[2:]:
        sums = sum_stage(sums.astype(BF16), bits)

    grad_back, out_feat = lax.optimization_barrier((grad_back, out_feat))

    grad_part = pl.pallas_call(
        last_kernel,
        out_shape=pltpu.VMEM((blocks, width, hidden), BF16),
        in_specs=[SMEM] + [VMEM] * 4,
        out_specs=VMEM,
        scratch_shapes=[pltpu.VMEM((blocks, width, hidden), F32)],
        compiler_params=params,
        name="owner_last",
    )(send_all, grad_back, grad_pre, w_self, w_msg)
    grad_pieces, sums, other = pieces_feat(grad_part, sums)
    grad_feat, grad_wself, grad_wmsg = join_feat(grad_pieces, [sums, other], params)
    return (out_feat, grad_feat, grad_wmsg, grad_wself)


def solution(mesh):
    in_specs = (
        P("edge", None),
        P("edge", None),
        P(),
        P(),
        P("edge", "feat", None, None, None),
        P("edge", "feat", None),
        P("edge", "feat", None),
        P("edge", "feat", None, None),
        P("edge", "feat", None, None),
        P("edge", "feat"),
    )
    out_specs = (P("edge", None), P("edge", None), P(), P())
    return jax.shard_map(body, mesh=mesh, in_specs=in_specs, out_specs=out_specs, check_vma=False)
```

```python
import functools
import math

import jax
import jax.numpy as jnp
from jax import lax
from jax.experimental import pallas as pl
from jax.experimental.pallas import tpu as pltpu
from jax.sharding import PartitionSpec as P

BOTH = ("edge", "feat")
F32 = jnp.float32
BF16 = jnp.bfloat16
VMEM = pl.BlockSpec(memory_space=pltpu.VMEM)
SMEM = pl.BlockSpec(memory_space=pltpu.SMEM)
HBM = pl.BlockSpec(memory_space=pltpu.HBM)
ANY = pl.BlockSpec(memory_space=pl.ANY)


def is_pow2(n):
    return n & (n - 1) == 0


def swap(x, axis, bit):
    size = lax.axis_size(axis)
    return lax.ppermute(x, axis, [(j, j ^ bit) for j in range(size)])


def gather_feat(x):
    size = lax.axis_size("feat")
    if not is_pow2(size):
        return lax.all_gather(x, "feat", axis=0)
    me = lax.axis_index("feat")
    held = x[None]
    bit = 1
    while bit < size:
        other = swap(held, "feat", bit)
        mine_low = (me & bit) == 0
        held = jnp.where(
            mine_low, jnp.concatenate([held, other], 0), jnp.concatenate([other, held], 0)
        )
        bit *= 2
    return held


def pieces_feat(x, beside=None):
    top = lax.axis_size("feat") // 2
    low = [1 << n for n in range(top.bit_length() - 1)][::-1]

    def spread(base, value):
        held = {base: value}
        for bit in low:
            held.update({m | bit: swap(v, "feat", bit) for m, v in list(held.items())})
        return held

    far = swap(x, "feat", top) if top else None
    held, other = spread(0, x), None
    if beside is not None:
        far, other = lax.optimization_barrier((far, swap_all(beside, 1)))
    if top:
        held.update(spread(top, far))
    return [held[m] for m in sorted(held)], beside, other


def join_kernel(planes, bounce, *refs):
    me = lax.axis_index("feat")
    pieces, refs = refs[:planes], refs[planes:]
    if bounce:
        out, room, sems, in_sems = refs
        ins = [
            pltpu.make_async_copy(piece, room.at[n], in_sems.at[n])
            for n, piece in enumerate(pieces)
        ]
        for copy in ins:
            copy.start()
        copies = [(room.at[n], out.at[:, me ^ n]) for n in range(planes)]
    else:
        ins = []
        halves, (out, *sums, sems) = refs[:2], refs[2:]
        copies = [(piece, out.at[:, me ^ n]) for n, piece in enumerate(pieces)]
        for n, total in enumerate(sums):
            rows = total.shape[1]
            copies += [
                (half.at[n * rows : (n + 1) * rows], total.at[(me & 1) ^ m])
                for m, half in enumerate(halves)
            ]
    copies = [pltpu.make_async_copy(a, b, sems.at[n]) for n, (a, b) in enumerate(copies)]
    for n, copy in enumerate(copies):
        if bounce:
            ins[n].wait()
        copy.start()
    for copy in copies:
        copy.wait()


def join_feat(pieces, halves, params):
    blocks, width, hidden = pieces[0].shape
    planes = len(pieces)
    count = 2 * halves[0].shape[0] // hidden if halves else 0
    out_shape = [pltpu.HBM((blocks, planes, width, hidden), BF16)]
    out_shape += [pltpu.HBM((2, hidden // 2, hidden), F32)] * count
    scratch = [pltpu.SemaphoreType.DMA((planes + 2 * count,))]
    if not halves:
        pieces = [in_hbm(piece) for piece in pieces]
        scratch = [pltpu.VMEM((planes, blocks, width, hidden), BF16), *scratch * 2]
    joined = pl.pallas_call(
        functools.partial(join_kernel, planes, not halves),
        out_shape=out_shape,
        in_specs=[VMEM if halves else HBM] * planes + [VMEM] * len(halves),
        out_specs=[HBM] * len(out_shape),
        scratch_shapes=scratch,
        compiler_params=params,
        name="join_rows",
    )(*pieces, *halves)
    return [v.reshape(-1, hidden) for v in joined]


def stages_of(count):
    bits = [1 << n for n in range(count.bit_length() - 1)]
    return [bits[:1]] + [bits[n : n + 2] for n in range(1, len(bits), 2)]


def swap_all(x, mask):
    count = lax.axis_size(BOTH)
    return lax.ppermute(x, BOTH, [(j, j ^ mask) for j in range(count)])


def sum_stage(x, bits):
    terms = {0: x}
    for bit in bits:
        terms.update({m | bit: swap_all(x, m | bit) for m in list(terms)})
    held = [terms[m].astype(F32) for m in sorted(terms)]
    while len(held) > 1:
        held = [held[n] + held[n + 1] for n in range(0, len(held), 2)]
    return held[0]


def split_core(x, me):
    halves = x.reshape(2, -1, x.shape[-1])
    low = (me & 1) == 0
    mine = jnp.where(low, halves[0], halves[1])
    other = jnp.where(low, halves[1], halves[0])
    return mine + swap_all(other, 1)


def pick_kernel(masks, ids, rows, w_msg, w_self, *refs):
    n_send, peers = ids.shape
    *outs, w_msg_out, w_self_out, sems = refs
    me = lax.axis_index("edge")
    copies = [
        (rows.at[ids[j, me ^ mask]], out.at[j])
        for mask, out in zip(masks, outs)
        for j in range(n_send)
    ]
    copies += [(w_msg, w_msg_out), (w_self, w_self_out)]
    copies = [pltpu.make_async_copy(a, b, sems.at[n]) for n, (a, b) in enumerate(copies)]
    for copy in copies:
        copy.start()
    for copy in copies:
        copy.wait()


def pieces_of(masks, raw):
    me = lax.axis_index("edge")
    return [((me ^ mask) * rows.shape[0], rows) for mask, rows in zip(masks, raw)]


def mask_order(peers):
    return sorted(range(peers), key=lambda m: (-m.bit_length(), -m))


def fetch_kernel(quarter, *refs):
    *ins, out, sems = refs
    me = lax.axis_index("feat")
    copies = [
        pltpu.make_async_copy(
            a.at[:, me] if quarter else a, out.at[n] if quarter else out, sems.at[n]
        )
        for n, a in enumerate(ins)
    ]
    for copy in copies:
        copy.start()
    for copy in copies:
        copy.wait()


def fetch(quarter, arrays, dims, params, name):
    return pl.pallas_call(
        functools.partial(fetch_kernel, quarter),
        out_shape=pltpu.VMEM(dims, BF16),
        in_specs=[HBM] * len(arrays),
        out_specs=VMEM,
        scratch_shapes=[pltpu.SemaphoreType.DMA((len(arrays),))],
        compiler_params=params,
        cost_estimate=pl.CostEstimate(
            flops=0, bytes_accessed=4 * math.prod(dims), transcendentals=0
        ),
        name=name,
    )(*arrays)


def edge_loop(group, count, term, put):
    def step(turn, carry):
        ks = [turn * group + u for u in range(group)]
        terms = [term(k) for k in ks]
        for k, value in zip(ks, terms):
            put(k, k < count, value)
        return carry

    lax.fori_loop(0, (count + group - 1) // group, step, 0)


def copy_ids(pairs, sems):
    copies = [pltpu.make_async_copy(a, b, sems.at[n]) for n, (a, b) in enumerate(pairs)]
    for copy in copies:
        copy.start()
    return copies


def send_out(room, out, sems, p, size):
    copy = pltpu.make_async_copy(
        room.at[p * size : (p + 1) * size], out.at[p * size : (p + 1) * size], sems.at[p]
    )
    copy.start()
    return copy


def forward_kernel(
    group, masks, live, src_in, dst_in, w_msg, adj, *refs
):
    *raw, out, msgs, acc, room, src, dst, sems, out_sems = refs
    slots, block, hidden = msgs.shape
    per_owner, width = out.shape[1:3]
    planes = block // width
    ids = copy_ids([(src_in, src), (dst_in, dst)], sems)
    for first, rows in pieces_of(masks, raw):
        flat = rows[...].reshape(-1, hidden)
        piece = jnp.dot(flat, w_msg[...], preferred_element_type=F32).astype(BF16)
        msgs[pl.ds(first, rows.shape[0])] = piece.reshape(rows.shape)
    acc[...] = jnp.zeros_like(acc)
    for copy in ids:
        copy.wait()

    def term(k):
        return jnp.dot(adj[k], msgs[src[k]], preferred_element_type=F32)

    def put(k, alive, value):
        acc[jnp.where(alive, dst[k], slots)] += value

    edge_loop(group, live[0], term, put)
    copies = []
    for p in range(out.shape[0] // planes):
        for j in range(per_owner):
            for q in range(planes):
                room[p * planes + q, j] = acc[
                    p * per_owner + j, q * width : (q + 1) * width
                ].astype(BF16)
        copies.append(send_out(room, out, out_sems, p, planes))
    for copy in copies:
        copy.wait()


def owner_kernel(
    ids, got, rows, w_self, out_feat, grad_pre, out, w_part, agg, held, room, out_room, out_sems
):
    blocks, width, hidden = held.shape
    devices, per_owner = got.shape[:2]
    agg[...] = jnp.zeros_like(agg)
    for i in range(devices):
        for j in range(per_owner):
            agg[ids[i * per_owner + j]] += got[i, j].astype(F32)
    mine = rows[0].reshape(blocks * width, hidden)
    preact = jnp.dot(mine, w_self[...], preferred_element_type=F32)
    preact = preact + agg[...].reshape(blocks * width, hidden)
    sig = jax.nn.sigmoid(preact)
    grad = rows[1].reshape(blocks * width, hidden).astype(F32)
    grad = (grad * sig * (1.0 + preact * (1.0 - sig))).astype(BF16)
    held[...] = grad.reshape(blocks, width, hidden)
    copies = []
    peers = out_sems.shape[0] - 2
    size = devices // peers
    for p in range(peers):
        for i in range(p * size, (p + 1) * size):
            for j in range(per_owner):
                room[i, j] = held[ids[i * per_owner + j]]
        copies.append(send_out(room, out, out_sems, p, size))
    out_room[...] = (preact * sig).astype(BF16).reshape(blocks, width, hidden)
    for n, (a, b) in enumerate([(out_room, out_feat), (held, grad_pre)]):
        copies.append(pltpu.make_async_copy(a, b, out_sems.at[peers + n]))
        copies[-1].start()
    w_part[...] = lax.dot_general(
        mine, grad, (((0,), (0,)), ((), ())), preferred_element_type=F32
    )
    for copy in copies:
        copy.wait()


def backward_kernel(group, masks, live, src_in, dst_in, got, adj, *refs):
    *raw, out, w_part, turned, acc, room, src, dst, sems, out_sems = refs
    slots, hidden, block = acc.shape
    slots -= 1
    devices, per_owner, width = got.shape[:3]
    planes = block // width
    out_slots = out.shape[1]
    ids = copy_ids([(src_in, src), (dst_in, dst)], sems)
    for p in range(devices // planes):
        for j in range(per_owner):
            whole = jnp.concatenate([got[p * planes + q, j] for q in range(planes)], 0)
            turned[p * per_owner + j] = whole.T
    acc[...] = jnp.zeros_like(acc)
    for copy in ids:
        copy.wait()

    def term(k):
        return jnp.dot(turned[dst[k]], adj[k], preferred_element_type=F32)

    def put(k, alive, value):
        acc[jnp.where(alive, src[k], slots)] += value

    edge_loop(group, live[0], term, put)
    copies = []
    for p in range(devices // planes):
        for j in range(out_slots):
            back = acc[p * out_slots + j].astype(BF16).T
            for q in range(planes):
                room[p * planes + q, j] = back[q * width : (q + 1) * width]
        copies.append(send_out(room, out, out_sems, p, planes))
    total = jnp.zeros((hidden, hidden), F32)
    for first, rows in pieces_of(masks, raw):
        for s in range(rows.shape[0]):
            total += jnp.dot(acc[first + s].astype(BF16), rows[s], preferred_element_type=F32)
    w_part[...] = total.T
    for copy in copies:
        copy.wait()


def last_kernel(ids, got, grad_pre, w_self, w_msg, out, agg):
    blocks, width, hidden = grad_pre.shape
    devices, per_owner = got.shape[:2]
    agg[...] = jnp.zeros_like(agg)
    for i in range(devices):
        for j in range(per_owner):
            agg[ids[i * per_owner + j]] += got[i, j].astype(F32)
    grad_msg = agg[...].reshape(blocks * width, hidden).astype(BF16)
    turn = (((1,), (1,)), ((), ()))
    total = lax.dot_general(
        grad_pre[...].reshape(blocks * width, hidden),
        w_self[...],
        turn,
        preferred_element_type=F32,
    ) + lax.dot_general(grad_msg, w_msg[...], turn, preferred_element_type=F32)
    out[...] = total.astype(BF16).reshape(blocks, width, hidden)


def shape(dims, dtype):
    return jax.ShapeDtypeStruct(dims, dtype)


def in_hbm(x):
    return pltpu.with_memory_space_constraint(x, pltpu.HBM)


def body(
    node_feat, cotangent, w_msg, w_self, adjacency, edge_src, edge_dst, send_src, recv_dst, live
):
    block = adjacency.shape[-1]
    hidden = node_feat.shape[1]
    blocks = node_feat.shape[0] // block
    peers = lax.axis_size("edge")
    planes = lax.axis_size("feat")
    devices = peers * planes
    width = block // planes
    n_send = send_src.shape[-1]
    n_recv = recv_dst.shape[-1]
    adj = in_hbm(adjacency.reshape(-1, block, block))
    src = in_hbm(edge_src.reshape(-1))
    dst = in_hbm(edge_dst.reshape(-1))
    count = live.reshape(1)
    group = math.gcd(64, adj.shape[0])
    me = lax.axis_index("feat").reshape(1).astype(jnp.int32)
    params = pltpu.CompilerParams(vmem_limit_bytes=32 * 2**20)
    stages = stages_of(devices)

    ids = jnp.concatenate([send_src.reshape(peers, n_send), recv_dst.reshape(peers, n_recv)], 1)
    ids = gather_feat(ids).transpose(1, 0, 2)
    send_all = ids[:, :, :n_send].reshape(-1)
    recv_all = ids[:, :, n_send:].reshape(-1)

    square = pltpu.VMEM((hidden, hidden), BF16)
    sum_part = pltpu.VMEM((hidden, hidden), F32)
    recv_out = (devices, n_recv, width, hidden)
    send_out_dims = (devices, n_send, width, hidden)
    out_sems = pltpu.SemaphoreType.DMA((peers,))
    masks = mask_order(peers)
    few = (n_send, block, hidden)
    *outgoing, w_msg, w_self = pl.pallas_call(
        functools.partial(pick_kernel, masks),
        out_shape=[pltpu.VMEM(few, BF16)] * peers + [square, square],
        in_specs=[SMEM] + [HBM] * 3,
        out_specs=[VMEM] * (peers + 2),
        scratch_shapes=[pltpu.SemaphoreType.DMA((peers * n_send + 2,))],
        compiler_params=params,
        name="pick_rows",
    )(
        in_hbm(send_src.transpose(0, 1, 3, 2).reshape(n_send, peers)),
        in_hbm(node_feat.reshape(blocks, block, hidden)),
        in_hbm(w_msg),
        in_hbm(w_self),
    )
    raw = [swap(rows, "edge", mask) if mask else rows for mask, rows in zip(masks, outgoing)]

    adj = fetch(False, [adj], adj.shape, params, "fetch_edges")
    ids_room = [pltpu.SMEM(v.shape, v.dtype) for v in (src, dst)]
    ids_room.append(pltpu.SemaphoreType.DMA((2,)))
    partials = pl.pallas_call(
        functools.partial(forward_kernel, group, masks),
        out_shape=pltpu.HBM(recv_out, BF16),
        in_specs=[SMEM] + [HBM] * 2 + [VMEM] * (2 + len(raw)),
        out_specs=HBM,
        scratch_shapes=[
            pltpu.VMEM((peers * n_send, block, hidden), BF16),
            pltpu.VMEM((peers * n_recv + 1, block, hidden), F32),
            pltpu.VMEM(recv_out, BF16),
            *ids_room,
            out_sems,
        ],
        compiler_params=params,
        name="edge_forward",
    )(count, src, dst, w_msg, adj, *raw)
    wide_feat, wide_cot, partials = lax.optimization_barrier(
        (node_feat, cotangent, partials)
    )
    wide_feat = in_hbm(wide_feat.reshape(blocks, planes, width, hidden))
    wide_cot = in_hbm(wide_cot.reshape(blocks, planes, width, hidden))
    got = lax.all_to_all(partials, BOTH, 0, 0, tiled=True)
    rows = fetch(True, [wide_feat, wide_cot], (2, blocks, width, hidden), params, "fetch_rows")

    out_part, grad_pre, grad_out, wself_part = pl.pallas_call(
        owner_kernel,
        out_shape=(
            pltpu.HBM((blocks, width, hidden), BF16),
            pltpu.HBM((blocks, width, hidden), BF16),
            pltpu.HBM(recv_out, BF16),
            sum_part,
        ),
        in_specs=[SMEM] + [VMEM] * 3,
        out_specs=(HBM, HBM, HBM, VMEM),
        scratch_shapes=[
            pltpu.VMEM((blocks, width, hidden), F32),
            pltpu.VMEM((blocks, width, hidden), BF16),
            pltpu.VMEM(recv_out, BF16),
            pltpu.VMEM((blocks, width, hidden), BF16),
            pltpu.SemaphoreType.DMA((peers + 2,)),
        ],
        compiler_params=params,
        name="owner_dense",
    )(recv_all, got, rows, w_self)
    grad_in = lax.all_to_all(grad_out, BOTH, 0, 0, tiled=True)
    out_pieces, _, _ = pieces_feat(out_part)
    wself_part = split_core(wself_part, me)
    for bits in stages[1:2]:
        wself_part = sum_stage(wself_part, bits)
    grad_in, out_pieces, wself_part = lax.optimization_barrier(
        (grad_in, out_pieces, wself_part)
    )

    grad_partials, wmsg_part = pl.pallas_call(
        functools.partial(backward_kernel, group, masks),
        out_shape=(pltpu.HBM(send_out_dims, BF16), sum_part),
        in_specs=[SMEM] + [HBM] * 2 + [VMEM] * (2 + len(raw)),
        out_specs=(HBM, VMEM),
        scratch_shapes=[
            pltpu.VMEM((peers * n_recv, hidden, block), BF16),
            pltpu.VMEM((peers * n_send + 1, hidden, block), F32),
            pltpu.VMEM(send_out_dims, BF16),
            *ids_room,
            out_sems,
        ],
        compiler_params=params,
        name="edge_backward",
    )(count, src, dst, grad_in, adj, *raw)
    grad_partials, wmsg_part, wself_part, out_pieces = lax.optimization_barrier(
        (grad_partials, wmsg_part, wself_part, out_pieces)
    )
    (out_feat,) = join_feat(out_pieces, [], params)
    grad_back = lax.all_to_all(grad_partials, BOTH, 0, 0, tiled=True)
    wmsg_part = split_core(wmsg_part, me)
    for bits in stages[1:2]:
        wmsg_part = sum_stage(wmsg_part, bits)
    sums = jnp.concatenate([wself_part, wmsg_part], 0)
    for bits in stages[2:]:
        sums = sum_stage(sums.astype(BF16), bits)

    grad_back, out_feat = lax.optimization_barrier((grad_back, out_feat))

    grad_part = pl.pallas_call(
        last_kernel,
        out_shape=pltpu.VMEM((blocks, width, hidden), BF16),
        in_specs=[SMEM] + [VMEM] * 4,
        out_specs=VMEM,
        scratch_shapes=[pltpu.VMEM((blocks, width, hidden), F32)],
        compiler_params=params,
        name="owner_last",
    )(send_all, grad_back, grad_pre, w_self, w_msg)
    grad_pieces, sums, other = pieces_feat(grad_part, sums)
    grad_feat, grad_wself, grad_wmsg = join_feat(grad_pieces, [sums, other], params)
    return (out_feat, grad_feat, grad_wmsg, grad_wself)


def solution(mesh):
    in_specs = (
        P("edge", None),
        P("edge", None),
        P(),
        P(),
        P("edge", "feat", None, None, None),
        P("edge", "feat", None),
        P("edge", "feat", None),
        P("edge", "feat", None, None),
        P("edge", "feat", None, None),
        P("edge", "feat"),
    )
    out_specs = (P("edge", None), P("edge", None), P(), P())
    return jax.shard_map(body, mesh=mesh, in_specs=in_specs, out_specs=out_specs, check_vma=False)
```

```python
import functools
import math

import jax
import jax.numpy as jnp
from jax import lax
from jax.experimental import pallas as pl
from jax.experimental.pallas import tpu as pltpu
from jax.sharding import PartitionSpec as P

BOTH = ("edge", "feat")
F32 = jnp.float32
BF16 = jnp.bfloat16
VMEM = pl.BlockSpec(memory_space=pltpu.VMEM)
SMEM = pl.BlockSpec(memory_space=pltpu.SMEM)
HBM = pl.BlockSpec(memory_space=pltpu.HBM)
ANY = pl.BlockSpec(memory_space=pl.ANY)


def is_pow2(n):
    return n & (n - 1) == 0


def swap(x, axis, bit):
    size = lax.axis_size(axis)
    return lax.ppermute(x, axis, [(j, j ^ bit) for j in range(size)])


def gather_feat(x):
    size = lax.axis_size("feat")
    if not is_pow2(size):
        return lax.all_gather(x, "feat", axis=0)
    me = lax.axis_index("feat")
    held = x[None]
    bit = 1
    while bit < size:
        other = swap(held, "feat", bit)
        mine_low = (me & bit) == 0
        held = jnp.where(
            mine_low, jnp.concatenate([held, other], 0), jnp.concatenate([other, held], 0)
        )
        bit *= 2
    return held


def pieces_feat(x, beside=None, along=None):
    top = lax.axis_size("feat") // 2
    low = [1 << n for n in range(top.bit_length() - 1)][::-1]

    def spread(base, value):
        held = {base: value}
        for bit in low:
            held.update({m | bit: swap(v, "feat", bit) for m, v in list(held.items())})
        return held

    far = swap(x, "feat", top) if top else None
    held, other = spread(0, x), None
    if beside is not None:
        far, other, along = lax.optimization_barrier((far, swap_all(beside, 1), along))
    if top:
        held.update(spread(top, far))
    return [held[m] for m in sorted(held)], beside, other, along


def join_kernel(planes, bounce, *refs):
    me = lax.axis_index("feat")
    pieces, refs = refs[:planes], refs[planes:]
    if bounce:
        out, room, sems, in_sems = refs
        ins = [
            pltpu.make_async_copy(piece, room.at[n], in_sems.at[n])
            for n, piece in enumerate(pieces)
        ]
        for copy in ins:
            copy.start()
        copies = [(room.at[n], out.at[:, me ^ n]) for n in range(planes)]
    else:
        ins = []
        halves, (out, *sums, sems) = refs[:2], refs[2:]
        copies = [(piece, out.at[:, me ^ n]) for n, piece in enumerate(pieces)]
        for n, total in enumerate(sums):
            rows = total.shape[1]
            copies += [
                (half.at[n * rows : (n + 1) * rows], total.at[(me & 1) ^ m])
                for m, half in enumerate(halves)
            ]
    copies = [pltpu.make_async_copy(a, b, sems.at[n]) for n, (a, b) in enumerate(copies)]
    for n, copy in enumerate(copies):
        if bounce:
            ins[n].wait()
        copy.start()
    for copy in copies:
        copy.wait()


def join_feat(pieces, halves, params):
    blocks, width, hidden = pieces[0].shape
    planes = len(pieces)
    count = 2 * halves[0].shape[0] // hidden if halves else 0
    out_shape = [pltpu.HBM((blocks, planes, width, hidden), BF16)]
    out_shape += [pltpu.HBM((2, hidden // 2, hidden), F32)] * count
    scratch = [pltpu.SemaphoreType.DMA((planes + 2 * count,))]
    if not halves:
        pieces = [in_hbm(piece) for piece in pieces]
        scratch = [pltpu.VMEM((planes, blocks, width, hidden), BF16), *scratch * 2]
    joined = pl.pallas_call(
        functools.partial(join_kernel, planes, not halves),
        out_shape=out_shape,
        in_specs=[VMEM if halves else HBM] * planes + [VMEM] * len(halves),
        out_specs=[HBM] * len(out_shape),
        scratch_shapes=scratch,
        compiler_params=params,
        name="join_rows",
    )(*pieces, *halves)
    return [v.reshape(-1, hidden) for v in joined]


def stages_of(count):
    bits = [1 << n for n in range(count.bit_length() - 1)]
    return [bits[:1]] + [bits[n : n + 2] for n in range(1, len(bits), 2)]


def swap_all(x, mask):
    count = lax.axis_size(BOTH)
    return lax.ppermute(x, BOTH, [(j, j ^ mask) for j in range(count)])


def sum_stage(x, bits):
    terms = {0: x}
    for bit in bits:
        terms.update({m | bit: swap_all(x, m | bit) for m in list(terms)})
    held = [terms[m].astype(F32) for m in sorted(terms)]
    while len(held) > 1:
        held = [held[n] + held[n + 1] for n in range(0, len(held), 2)]
    return held[0]


def split_core(x, me):
    halves = x.reshape(2, -1, x.shape[-1])
    low = (me & 1) == 0
    mine = jnp.where(low, halves[0], halves[1])
    other = jnp.where(low, halves[1], halves[0])
    return mine + swap_all(other, 1)


def pick_kernel(masks, ids, rows, w_msg, w_self, *refs):
    n_send, peers = ids.shape
    *outs, w_msg_out, w_self_out, sems = refs
    me = lax.axis_index("edge")
    copies = [
        (rows.at[ids[j, me ^ mask]], out.at[j])
        for mask, out in zip(masks, outs)
        for j in range(n_send)
    ]
    copies += [(w_msg, w_msg_out), (w_self, w_self_out)]
    copies = [pltpu.make_async_copy(a, b, sems.at[n]) for n, (a, b) in enumerate(copies)]
    for copy in copies:
        copy.start()
    for copy in copies:
        copy.wait()


def pieces_of(masks, raw):
    me = lax.axis_index("edge")
    return [((me ^ mask) * rows.shape[0], rows) for mask, rows in zip(masks, raw)]


def mask_order(peers):
    return sorted(range(peers), key=lambda m: (-m.bit_length(), -m))


def fetch_kernel(quarter, *refs):
    *ins, out, sems = refs
    me = lax.axis_index("feat")
    copies = [
        pltpu.make_async_copy(
            a.at[:, me] if quarter else a, out.at[n] if quarter else out, sems.at[n]
        )
        for n, a in enumerate(ins)
    ]
    for copy in copies:
        copy.start()
    for copy in copies:
        copy.wait()


def fetch(quarter, arrays, dims, params, name):
    return pl.pallas_call(
        functools.partial(fetch_kernel, quarter),
        out_shape=pltpu.VMEM(dims, BF16),
        in_specs=[HBM] * len(arrays),
        out_specs=VMEM,
        scratch_shapes=[pltpu.SemaphoreType.DMA((len(arrays),))],
        compiler_params=params,
        cost_estimate=pl.CostEstimate(
            flops=0, bytes_accessed=4 * math.prod(dims), transcendentals=0
        ),
        name=name,
    )(*arrays)


def edge_loop(group, count, term, put):
    def step(turn, carry):
        ks = [turn * group + u for u in range(group)]
        terms = [term(k) for k in ks]
        for k, value in zip(ks, terms):
            put(k, k < count, value)
        return carry

    lax.fori_loop(0, (count + group - 1) // group, step, 0)


def copy_ids(pairs, sems):
    copies = [pltpu.make_async_copy(a, b, sems.at[n]) for n, (a, b) in enumerate(pairs)]
    for copy in copies:
        copy.start()
    return copies


def send_out(room, out, sems, p, size):
    copy = pltpu.make_async_copy(
        room.at[p * size : (p + 1) * size], out.at[p * size : (p + 1) * size], sems.at[p]
    )
    copy.start()
    return copy


def forward_kernel(
    group, masks, live, src_in, dst_in, w_msg, adj, *refs
):
    *raw, out, msgs, acc, room, src, dst, sems, out_sems = refs
    slots, block, hidden = msgs.shape
    per_owner, width = out.shape[1:3]
    planes = block // width
    ids = copy_ids([(src_in, src), (dst_in, dst)], sems)
    for first, rows in pieces_of(masks, raw):
        flat = rows[...].reshape(-1, hidden)
        piece = jnp.dot(flat, w_msg[...], preferred_element_type=F32).astype(BF16)
        msgs[pl.ds(first, rows.shape[0])] = piece.reshape(rows.shape)
    acc[...] = jnp.zeros_like(acc)
    for copy in ids:
        copy.wait()

    def term(k):
        return jnp.dot(adj[k], msgs[src[k]], preferred_element_type=F32)

    def put(k, alive, value):
        acc[jnp.where(alive, dst[k], slots)] += value

    edge_loop(group, live[0], term, put)
    copies = []
    for p in range(out.shape[0] // planes):
        for j in range(per_owner):
            for q in range(planes):
                room[p * planes + q, j] = acc[
                    p * per_owner + j, q * width : (q + 1) * width
                ].astype(BF16)
        copies.append(send_out(room, out, out_sems, p, planes))
    for copy in copies:
        copy.wait()


def owner_kernel(
    ids, got, rows, w_self, out_feat, grad_pre, out, w_part, agg, held, room, out_room, out_sems
):
    blocks, width, hidden = held.shape
    devices, per_owner = got.shape[:2]
    agg[...] = jnp.zeros_like(agg)
    for i in range(devices):
        for j in range(per_owner):
            agg[ids[i * per_owner + j]] += got[i, j].astype(F32)
    mine = rows[0].reshape(blocks * width, hidden)
    preact = jnp.dot(mine, w_self[...], preferred_element_type=F32)
    preact = preact + agg[...].reshape(blocks * width, hidden)
    sig = jax.nn.sigmoid(preact)
    grad = rows[1].reshape(blocks * width, hidden).astype(F32)
    grad = (grad * sig * (1.0 + preact * (1.0 - sig))).astype(BF16)
    held[...] = grad.reshape(blocks, width, hidden)
    copies = []
    peers = out_sems.shape[0] - 2
    size = devices // peers
    for p in range(peers):
        for i in range(p * size, (p + 1) * size):
            for j in range(per_owner):
                room[i, j] = held[ids[i * per_owner + j]]
        copies.append(send_out(room, out, out_sems, p, size))
    out_room[...] = (preact * sig).astype(BF16).reshape(blocks, width, hidden)
    for n, (a, b) in enumerate([(out_room, out_feat), (held, grad_pre)]):
        copies.append(pltpu.make_async_copy(a, b, out_sems.at[peers + n]))
        copies[-1].start()
    w_part[...] = lax.dot_general(
        mine, grad, (((0,), (0,)), ((), ())), preferred_element_type=F32
    )
    for copy in copies:
        copy.wait()


def backward_kernel(group, masks, live, src_in, dst_in, got, adj, *refs):
    *raw, out, w_part, turned, acc, room, src, dst, sems, out_sems = refs
    slots, hidden, block = acc.shape
    slots -= 1
    devices, per_owner, width = got.shape[:3]
    planes = block // width
    out_slots = out.shape[1]
    ids = copy_ids([(src_in, src), (dst_in, dst)], sems)
    for p in range(devices // planes):
        for j in range(per_owner):
            whole = jnp.concatenate([got[p * planes + q, j] for q in range(planes)], 0)
            turned[p * per_owner + j] = whole.T
    acc[...] = jnp.zeros_like(acc)
    for copy in ids:
        copy.wait()

    def term(k):
        return jnp.dot(turned[dst[k]], adj[k], preferred_element_type=F32)

    def put(k, alive, value):
        acc[jnp.where(alive, src[k], slots)] += value

    edge_loop(group, live[0], term, put)
    copies = []
    for p in range(devices // planes):
        for j in range(out_slots):
            back = acc[p * out_slots + j].astype(BF16).T
            for q in range(planes):
                room[p * planes + q, j] = back[q * width : (q + 1) * width]
        copies.append(send_out(room, out, out_sems, p, planes))
    total = jnp.zeros((hidden, hidden), F32)
    for first, rows in pieces_of(masks, raw):
        for s in range(rows.shape[0]):
            total += jnp.dot(acc[first + s].astype(BF16), rows[s], preferred_element_type=F32)
    w_part[...] = total.T
    for copy in copies:
        copy.wait()


def last_kernel(ids, got, grad_pre, w_self, w_msg, out, agg):
    blocks, width, hidden = grad_pre.shape
    devices, per_owner = got.shape[:2]
    agg[...] = jnp.zeros_like(agg)
    for i in range(devices):
        for j in range(per_owner):
            agg[ids[i * per_owner + j]] += got[i, j].astype(F32)
    grad_msg = agg[...].reshape(blocks * width, hidden).astype(BF16)
    turn = (((1,), (1,)), ((), ()))
    total = lax.dot_general(
        grad_pre[...].reshape(blocks * width, hidden),
        w_self[...],
        turn,
        preferred_element_type=F32,
    ) + lax.dot_general(grad_msg, w_msg[...], turn, preferred_element_type=F32)
    out[...] = total.astype(BF16).reshape(blocks, width, hidden)


def shape(dims, dtype):
    return jax.ShapeDtypeStruct(dims, dtype)


def in_hbm(x):
    return pltpu.with_memory_space_constraint(x, pltpu.HBM)


def body(
    node_feat, cotangent, w_msg, w_self, adjacency, edge_src, edge_dst, send_src, recv_dst, live
):
    block = adjacency.shape[-1]
    hidden = node_feat.shape[1]
    blocks = node_feat.shape[0] // block
    peers = lax.axis_size("edge")
    planes = lax.axis_size("feat")
    devices = peers * planes
    width = block // planes
    n_send = send_src.shape[-1]
    n_recv = recv_dst.shape[-1]
    adj = in_hbm(adjacency.reshape(-1, block, block))
    src = in_hbm(edge_src.reshape(-1))
    dst = in_hbm(edge_dst.reshape(-1))
    count = live.reshape(1)
    group = math.gcd(64, adj.shape[0])
    me = lax.axis_index("feat").reshape(1).astype(jnp.int32)
    params = pltpu.CompilerParams(vmem_limit_bytes=32 * 2**20)
    stages = stages_of(devices)

    ids = jnp.concatenate([send_src.reshape(peers, n_send), recv_dst.reshape(peers, n_recv)], 1)
    ids = gather_feat(ids).transpose(1, 0, 2)
    send_all = ids[:, :, :n_send].reshape(-1)
    recv_all = ids[:, :, n_send:].reshape(-1)

    square = pltpu.VMEM((hidden, hidden), BF16)
    sum_part = pltpu.VMEM((hidden, hidden), F32)
    recv_out = (devices, n_recv, width, hidden)
    send_out_dims = (devices, n_send, width, hidden)
    out_sems = pltpu.SemaphoreType.DMA((peers,))
    masks = mask_order(peers)
    few = (n_send, block, hidden)
    *outgoing, w_msg, w_self = pl.pallas_call(
        functools.partial(pick_kernel, masks),
        out_shape=[pltpu.VMEM(few, BF16)] * peers + [square, square],
        in_specs=[SMEM] + [HBM] * 3,
        out_specs=[VMEM] * (peers + 2),
        scratch_shapes=[pltpu.SemaphoreType.DMA((peers * n_send + 2,))],
        compiler_params=params,
        name="pick_rows",
    )(
        in_hbm(send_src.transpose(0, 1, 3, 2).reshape(n_send, peers)),
        in_hbm(node_feat.reshape(blocks, block, hidden)),
        in_hbm(w_msg),
        in_hbm(w_self),
    )
    raw = [swap(rows, "edge", mask) if mask else rows for mask, rows in zip(masks, outgoing)]

    adj = fetch(False, [adj], adj.shape, params, "fetch_edges")
    ids_room = [pltpu.SMEM(v.shape, v.dtype) for v in (src, dst)]
    ids_room.append(pltpu.SemaphoreType.DMA((2,)))
    partials = pl.pallas_call(
        functools.partial(forward_kernel, group, masks),
        out_shape=pltpu.HBM(recv_out, BF16),
        in_specs=[SMEM] + [HBM] * 2 + [VMEM] * (2 + len(raw)),
        out_specs=HBM,
        scratch_shapes=[
            pltpu.VMEM((peers * n_send, block, hidden), BF16),
            pltpu.VMEM((peers * n_recv + 1, block, hidden), F32),
            pltpu.VMEM(recv_out, BF16),
            *ids_room,
            out_sems,
        ],
        compiler_params=params,
        name="edge_forward",
    )(count, src, dst, w_msg, adj, *raw)
    wide_feat, wide_cot, partials = lax.optimization_barrier(
        (node_feat, cotangent, partials)
    )
    wide_feat = in_hbm(wide_feat.reshape(blocks, planes, width, hidden))
    wide_cot = in_hbm(wide_cot.reshape(blocks, planes, width, hidden))
    got = lax.all_to_all(partials, BOTH, 0, 0, tiled=True)
    rows = fetch(True, [wide_feat, wide_cot], (2, blocks, width, hidden), params, "fetch_rows")

    out_part, grad_pre, grad_out, wself_part = pl.pallas_call(
        owner_kernel,
        out_shape=(
            pltpu.HBM((blocks, width, hidden), BF16),
            pltpu.HBM((blocks, width, hidden), BF16),
            pltpu.HBM(recv_out, BF16),
            sum_part,
        ),
        in_specs=[SMEM] + [VMEM] * 3,
        out_specs=(HBM, HBM, HBM, VMEM),
        scratch_shapes=[
            pltpu.VMEM((blocks, width, hidden), F32),
            pltpu.VMEM((blocks, width, hidden), BF16),
            pltpu.VMEM(recv_out, BF16),
            pltpu.VMEM((blocks, width, hidden), BF16),
            pltpu.SemaphoreType.DMA((peers + 2,)),
        ],
        compiler_params=params,
        name="owner_dense",
    )(recv_all, got, rows, w_self)
    grad_in = lax.all_to_all(grad_out, BOTH, 0, 0, tiled=True)
    out_pieces = pieces_feat(out_part)[0]
    wself_part = split_core(wself_part, me)
    for bits in stages[1:2]:
        wself_part = sum_stage(wself_part, bits)
    grad_in, out_pieces, wself_part = lax.optimization_barrier(
        (grad_in, out_pieces, wself_part)
    )

    grad_partials, wmsg_part = pl.pallas_call(
        functools.partial(backward_kernel, group, masks),
        out_shape=(pltpu.HBM(send_out_dims, BF16), sum_part),
        in_specs=[SMEM] + [HBM] * 2 + [VMEM] * (2 + len(raw)),
        out_specs=(HBM, VMEM),
        scratch_shapes=[
            pltpu.VMEM((peers * n_recv, hidden, block), BF16),
            pltpu.VMEM((peers * n_send + 1, hidden, block), F32),
            pltpu.VMEM(send_out_dims, BF16),
            *ids_room,
            out_sems,
        ],
        compiler_params=params,
        name="edge_backward",
    )(count, src, dst, grad_in, adj, *raw)
    grad_partials, wmsg_part, wself_part, out_pieces = lax.optimization_barrier(
        (grad_partials, wmsg_part, wself_part, out_pieces)
    )
    grad_back = lax.all_to_all(grad_partials, BOTH, 0, 0, tiled=True)
    wmsg_part = split_core(wmsg_part, me)
    for bits in stages[1:2]:
        wmsg_part = sum_stage(wmsg_part, bits)
    sums = jnp.concatenate([wself_part, wmsg_part], 0)
    last = [bit for bits in stages[2:] for bit in bits]
    for bit in last[:-1]:
        sums = sum_stage(sums, [bit])
    for bit in last[-1:]:
        sums = sum_stage(sums.astype(BF16), [bit])

    grad_part = pl.pallas_call(
        last_kernel,
        out_shape=pltpu.VMEM((blocks, width, hidden), BF16),
        in_specs=[SMEM] + [VMEM] * 4,
        out_specs=VMEM,
        scratch_shapes=[pltpu.VMEM((blocks, width, hidden), F32)],
        compiler_params=params,
        name="owner_last",
    )(send_all, grad_back, grad_pre, w_self, w_msg)
    grad_part, out_pieces = lax.optimization_barrier((grad_part, out_pieces))
    (out_feat,) = join_feat(out_pieces, [], params)
    grad_pieces, sums, other, out_feat = pieces_feat(grad_part, sums, out_feat)
    grad_feat, grad_wself, grad_wmsg = join_feat(grad_pieces, [sums, other], params)
    return (out_feat, grad_feat, grad_wmsg, grad_wself)


def solution(mesh):
    in_specs = (
        P("edge", None),
        P("edge", None),
        P(),
        P(),
        P("edge", "feat", None, None, None),
        P("edge", "feat", None),
        P("edge", "feat", None),
        P("edge", "feat", None, None),
        P("edge", "feat", None, None),
        P("edge", "feat"),
    )
    out_specs = (P("edge", None), P("edge", None), P(), P())
    return jax.shard_map(body, mesh=mesh, in_specs=in_specs, out_specs=out_specs, check_vma=False)
```
